256 devices in a mesh: stn: 128 (over y_lo, z, x, core), tpl: 2 (over y_hi).
Axes of the slice: x: 4, y: 4 (y_hi: 2, y_lo: 2; y = y_hi * 2 + y_lo), z: 8, core: 2. Of those that a mesh axis runs over, the one named last changes fastest.
Arguments:
- archive: bfloat16 [8192, 17408], P('stn'), may hold values from -400 to 400
- slot_of_row: int32 [8192], P('stn'), may hold values from 0 to 8191, as said below
- templates: bfloat16 [64, 30, 600], P('tpl'), may hold values from -5 to 5
- template_channels: int32 [64, 30], P('tpl'), may hold values from 0 to 8191, as said below
- moveouts: int32 [64, 30], P('tpl'), may hold values from 0 to 384, as said below
Outputs:
- grouped: bfloat16 [8192, 17408], P('stn')
- stack: float32 [64, 16384], P('tpl', 'stn')
The draws below stay inside these ranges and needn't reach their ends.
Inputs may be any that keep to these rules, and one draw needn't show every extreme that they name: `slot_of_row`: A permutation: channel p in owner order belongs to index p // 64 of stn. Of the 64 rows held by one index of stn, at most 2 go to any one owner, and in every draw some owner receives exactly 2 of them. `template_channels`: among the templates of one index of tpl, at most 22 entries name channels of any one owner, and one owner is named exactly 22 times. `moveouts`: the first channel of every template has moveout 0; some entry equals 384.
All inputs are finite; a program needn't handle non-finite values.
Results may differ from the reference program's by a relative error of at most 0.001.
Values may be sent and summed in bfloat16 or wider, within the bound.
No kernel may reach another device: no remote copies, remote signals or barrier semaphores. Data moves between devices by JAX's collectives and lax.ppermute only.
A program may use at most 128 MiB of HBM per device.

```python
import math
import jax
import jax.numpy as jnp
from jax import lax

M = 64
C = 30
TLEN = 600
MVMAX = 384
CH_DEV = 64
L = 16384
NT = 17408
CHANNELS = 8192
CAP = 2
KMAX = 22
N_STN = 128
N_TPL = 2


def draw_slot_of_row(key, part):
    key = jax.random.fold_in(key, 11)
    key_offsets, key_source, key_owner = jax.random.split(key, 3)
    offsets = jax.random.permutation(key_offsets, N_STN).astype(jnp.int32)
    half_count = CH_DEV // 2
    index_row = jnp.arange(CH_DEV, dtype=jnp.int32)
    group_of = jnp.where(index_row < half_count, index_row // CAP, half_count // CAP + (index_row - half_count) // max(1, CAP // 2))
    shift_of = offsets[group_of]
    sources = jnp.arange(N_STN, dtype=jnp.int32)[:, None]
    owners = (sources + shift_of[None, :]) % N_STN
    source_perm = jax.vmap(lambda sub_key: jax.random.permutation(sub_key, CH_DEV))(jax.random.split(key_source, N_STN)).astype(jnp.int32)
    owner_perm = jax.vmap(lambda sub_key: jax.random.permutation(sub_key, CH_DEV))(jax.random.split(key_owner, N_STN)).astype(jnp.int32)
    slots = owners * CH_DEV + owner_perm[owners, index_row[None, :]]
    archive_pos = sources * CH_DEV + source_perm
    return jnp.zeros((CHANNELS,), jnp.int32).at[archive_pos.reshape(-1)].set(slots.reshape(-1))


def draw_template_channels(key, part):
    key = jax.random.fold_in(key, 12)
    per_half = M // N_TPL * C

    def one_half(half_key):
        key_rank, key_crowd, key_rows = jax.random.split(half_key, 3)
        ranking = jax.random.permutation(key_rank, per_half).astype(jnp.int32)
        crowded = jax.random.randint(key_crowd, (), 0, N_STN)
        spread_owner = (crowded + 1 + (ranking - KMAX) % (N_STN - 1)) % N_STN
        owners = jnp.where(ranking < KMAX, crowded, spread_owner)
        row_pick = jax.random.randint(key_rows, (per_half,), 0, CH_DEV)
        return owners * CH_DEV + row_pick
    halves = jax.vmap(one_half)(jax.random.split(key, N_TPL))
    return halves.reshape(M, C).astype(jnp.int32)


def draw_moveouts(key, part):
    key = jax.random.fold_in(key, 13)
    key_values, key_template, key_channel = jax.random.split(key, 3)
    values = jax.random.randint(key_values, (M, C), 0, MVMAX + 1)
    values = values.at[:, 0].set(0)
    which_template = jax.random.randint(key_template, (), 0, M)
    which_channel = jax.random.randint(key_channel, (), 1, C)
    return values.at[which_template, which_channel].set(MVMAX).astype(jnp.int32)


def draw_archive(key, part):
    key = jax.random.fold_in(key, 14)
    key_base, key_gain, key_env = jax.random.split(key, 3)
    base = jax.random.truncated_normal(key_base, -5.0, 5.0, (CHANNELS, NT), jnp.float32)
    env_top = math.log(4.0)
    row_gain = jnp.exp(jax.random.uniform(key_gain, (CHANNELS, 1), jnp.float32) * math.log(10.0))
    blocks = jnp.exp(jax.random.uniform(key_env, (CHANNELS, NT // 128, 1), jnp.float32) * env_top)
    envelope = jnp.broadcast_to(blocks, (CHANNELS, NT // 128, 128)).reshape(CHANNELS, NT)
    return (base * row_gain * envelope).astype(jnp.bfloat16)


def block_scale(own_key, extent, cuts, least, top_value):
    def one(axis_at, blocks):
        heights = jax.random.uniform(jax.random.fold_in(jax.random.fold_in(own_key, 6), axis_at), (blocks,), jnp.float32, least / len(cuts), top_value / len(cuts))
        return jnp.repeat(jnp.exp(heights), extent[axis_at] // blocks).reshape((-1,) + (1,) * (len(extent) - axis_at - 1))

    factor_of = one(*cuts[0])
    for cut in cuts[1:]:
        factor_of = factor_of * one(*cut)
    return factor_of


def scatter_about(rng, shape, deviation, limit, shards=(), kind=jnp.bfloat16):
    factor_of = block_scale(rng, shape, shards, -0.22, 0.18) if shards else 1.0
    entries = jax.random.normal(rng, shape, jnp.float32) * deviation * factor_of
    return jnp.minimum(jnp.maximum(entries, -limit), limit).astype(kind)


def setup_inputs(seed: int = 0) -> dict:
    streams_of = jax.random.split(jax.random.key(seed), 6)
    archive = draw_archive(jax.random.fold_in(streams_of[5], 71), 0)
    slot_of_row = draw_slot_of_row(jax.random.fold_in(streams_of[5], 71), 0)
    templates = scatter_about(streams_of[2], (M, C, TLEN), 1.0, 5.0, ((0, 2),))
    template_channels = draw_template_channels(jax.random.fold_in(streams_of[5], 71), 0)
    moveouts = draw_moveouts(jax.random.fold_in(streams_of[5], 71), 0)
    return {"archive": archive, "slot_of_row": slot_of_row, "templates": templates, "template_channels": template_channels, "moveouts": moveouts}


EPSILON = 1e-06

def take_lags(series, lag_shift):
    return lax.dynamic_slice_in_dim(series, lag_shift, L)

def per_template(grouped, waveform, channel_ids, shifts):
    span = L + MVMAX
    channel_rows = grouped[channel_ids, :span + TLEN - 1].astype(jnp.float32)
    kernel = waveform.astype(jnp.float32)[:, None, :]
    correlation = lax.conv_general_dilated(channel_rows[None], kernel, (1,), 'VALID', feature_group_count=C, precision=lax.Precision.HIGHEST)[0]
    energy = lax.reduce_window(channel_rows * channel_rows, jnp.zeros((), channel_rows.dtype), lax.add, (1, TLEN), (1, 1), 'VALID')
    wave_full = waveform.astype(jnp.float32)
    template_power = lax.optimization_barrier(jnp.sum(wave_full * wave_full, axis=1))
    normalized = correlation / TLEN / jnp.sqrt((energy / TLEN + EPSILON) * (template_power[:, None] / TLEN + EPSILON))
    aligned = jax.vmap(take_lags)(normalized, shifts)
    return lax.optimization_barrier(jnp.sum(aligned, axis=0)) * math.sqrt(TLEN / C)

def reference(archive, slot_of_row, templates, template_channels, moveouts):
    grouped = jnp.zeros_like(archive).at[slot_of_row].set(archive)
    stack = lax.map(lambda packed: per_template(grouped, packed[0], packed[1], packed[2]), (templates, template_channels, moveouts))
    return (grouped, stack)
```

```python
import functools
import math

import jax
import jax.numpy as jnp
from jax import lax
from jax.experimental import pallas as pl
from jax.experimental.pallas import tpu as pltpu
from jax.sharding import PartitionSpec as P

EPSILON = 1e-06
LANES = 128
KW = 7
SPAN = KW * LANES
VMEM_LIMIT = 60 * 1024 * 1024


def roll_half(x):
    return pltpu.roll(x, LANES // 2, 1)


def left_lanes(rows):
    return lax.broadcasted_iota(jnp.int32, (rows, LANES), 1) < LANES // 2


def pack_kernel(half_ref, base_ref, info_ref, archive_ref, out_ref, tail_ref, *, rows, tiles, tail_tiles):
    which = half_ref[0]
    half = rows // 2
    left = left_lanes(half)
    owners = out_ref.shape[0]
    tail_lines = 2 * tail_tiles
    tail_ref[...] = jnp.zeros_like(tail_ref)
    tail_start = 2 * tiles * LANES
    info = info_ref[...]
    for tile in range(tail_tiles):
        at = pl.multiple_of(tail_start + (which * tail_tiles + tile) * LANES, LANES)
        block = archive_ref[:, pl.ds(at, LANES)].astype(jnp.float32)
        for row in range(rows):
            tail_ref[pl.ds(base_ref[row] * tail_tiles + tile, 1), :] = block[row : row + 1, :]

    def one(tile, carry):
        at = pl.multiple_of((which * tiles + tile) * LANES, LANES)
        block = archive_ref[:, pl.ds(at, LANES)].astype(jnp.float32)
        upper, lower = block[:half], block[half:]
        even = jnp.where(left, upper, roll_half(lower))
        odd = jnp.where(left, roll_half(upper), lower)
        for side, lines in ((0, even), (1, odd)):
            owner = 2 * tile + side
            tail = tail_ref[pl.ds(pl.multiple_of(owner * tail_lines, 8), tail_lines), :]
            out_ref[owner] = jnp.concatenate([lines, tail, info], axis=0).astype(jnp.bfloat16)
        return carry

    lax.fori_loop(0, owners // 2, one, 0, unroll=8)


def permute_kernel(
    owner_ref, got_ref, out_ref, tail_out_ref,
    plain_ref, placed_ref, tail_ref, tail_rows_ref, info_ref, route_ref, keep_ref,
    route_smem, keep_smem, route_sem, keep_sem, *, rows, tail_tiles,
):
    stations = got_ref.shape[0]
    half = rows // 2
    left = left_lanes(half)
    tail_lines = 2 * tail_tiles
    swapped = stations * half

    def note(station, carry):
        info_ref[pl.ds(station, 1), :] = got_ref[station][half + tail_lines : half + tail_lines + 8].astype(
            jnp.float32
        )[:1]
        return carry

    lax.fori_loop(0, stations, note, 0, unroll=8)
    info = info_ref[...].astype(jnp.int32)
    other = pltpu.roll(info_ref[...], rows, 1).astype(jnp.int32)
    lane = lax.broadcasted_iota(jnp.int32, info.shape, 1)
    station = lax.broadcasted_iota(jnp.int32, info.shape, 0)
    on_left = lane < rows
    target = jnp.where(on_left, info, other)
    packed = jnp.where(on_left, other, info)
    place, rank = packed % rows, packed // rows
    row = lane % rows
    crossed = (place // half) != (row // half)
    source = station * half + row % half + jnp.where(crossed, swapped, 0)
    route_ref[...] = jnp.where(on_left, target * rows + place, source)
    mine = target == owner_ref[0]
    side = jnp.where(on_left, 0, 1)
    first = jnp.max(jnp.where(mine & (rank == 0), place, -1), axis=1, keepdims=True)
    second = jnp.max(jnp.where(mine & (rank == 1), place, -1), axis=1, keepdims=True)
    kept = jnp.where(side == 0, first, second)
    keep_ref[...] = jnp.where(kept < 0, rows, kept)
    route_copy = pltpu.make_async_copy(route_ref, route_smem, route_sem)
    keep_copy = pltpu.make_async_copy(keep_ref, keep_smem, keep_sem)
    route_copy.start()
    keep_copy.start()

    def expand(station, carry):
        block = got_ref[station].astype(jnp.float32)
        lines = block[:half]
        at = pl.multiple_of(station * half, 8)
        plain_ref[pl.ds(at, half), :] = lines
        plain_ref[pl.ds(swapped + at, half), :] = roll_half(lines)
        tail_ref[pl.ds(pl.multiple_of(station * tail_lines, 8), tail_lines), :] = block[half : half + tail_lines]
        return carry

    lax.fori_loop(0, stations, expand, 0, unroll=8)
    route_copy.wait()
    keep_copy.wait()

    def move(station, carry):
        for row in range(rows):
            placed_ref[pl.ds(route_smem[station, row], 1), :] = plain_ref[
                pl.ds(route_smem[station, rows + row], 1), :
            ]
        return carry

    lax.fori_loop(0, stations, move, 0)

    def keep(station, carry):
        for rank in range(2):
            row = keep_smem[station, rank * rows]
            for tile in range(tail_tiles):
                line = station * tail_lines + rank * tail_tiles + tile
                tail_rows_ref[tile, pl.ds(row, 1), :] = tail_ref[pl.ds(line, 1), :]
        return carry

    lax.fori_loop(0, stations, keep, 0, unroll=8)
    for tile in range(tail_tiles):
        tail_out_ref[:, tile * LANES : (tile + 1) * LANES] = tail_rows_ref[tile, :rows, :].astype(jnp.bfloat16)

    def join(station, carry):
        at = pl.multiple_of(station * rows, 8)
        lines = jnp.where(left, placed_ref[pl.ds(at, half), :], placed_ref[pl.ds(at + half, half), :])
        lines = lines.astype(jnp.bfloat16)
        out_ref[2 * station] = lines
        out_ref[2 * station + 1] = lines
        return carry

    lax.fori_loop(0, stations, join, 0, unroll=8)


def assemble_kernel(got_ref, tail_low_ref, tail_high_ref, out_ref, *, tiles):
    half = got_ref.shape[1]
    left = left_lanes(half)
    for which in range(2):

        def one(tile, carry, which=which):
            even = got_ref[4 * tile + which].astype(jnp.float32)
            odd = got_ref[4 * tile + 2 + which].astype(jnp.float32)
            upper = jnp.where(left, even, roll_half(odd))
            lower = jnp.where(left, roll_half(even), odd)
            at = pl.multiple_of((which * tiles + tile) * LANES, LANES)
            out_ref[:, pl.ds(at, LANES)] = jnp.concatenate([upper, lower], axis=0).astype(jnp.bfloat16)
            return carry

        lax.fori_loop(0, tiles, one, 0, unroll=8)
    at = 2 * tiles * LANES
    width = tail_low_ref.shape[1]
    out_ref[:, at : at + width] = tail_low_ref[...]
    out_ref[:, at + width : at + 2 * width] = tail_high_ref[...]


def halving_bits(sizes):
    ys, zs, xs, cores = (size.bit_length() - 1 for size in sizes)
    x_from, z_from, y_from = cores, cores + xs, cores + xs + zs
    return (
        list(range(cores))
        + list(range(y_from, y_from + ys))
        + list(range(x_from, z_from))
        + list(reversed(range(z_from, y_from)))
    )


def place_of(index, bits):
    place = 0
    for at, bit in enumerate(bits):
        place = place + ((index >> bit) & 1) * (1 << (len(bits) - 1 - at))
    return place


def correlate_kernel(
    count_ref, entry_ref, row_ref, shift_ref, place_ref, archive_ref, wave_ref, out_ref,
    series_ref, line_ref, high_ref, low_ref, *, length, channels, bits,
):
    rows = archive_ref.shape[0]
    tiles = archive_ref.shape[1] // LANES
    blocks = LANES
    padded = series_ref.shape[0]

    def widen(tile, carry):
        at = pl.multiple_of(tile * LANES, LANES)
        series_ref[tile] = archive_ref[:, pl.ds(at, LANES)].astype(jnp.float32)
        return carry

    lax.fori_loop(0, tiles, widen, 0, unroll=8)
    for tile in range(tiles, padded):
        series_ref[tile] = jnp.zeros((rows, LANES), jnp.float32)
    out_ref[...] = jnp.zeros_like(out_ref)
    line_ref[...] = jnp.zeros_like(line_ref)
    my_place = place_ref[0]
    lag = lax.broadcasted_iota(jnp.int32, (LANES, SPAN), 1) - lax.broadcasted_iota(jnp.int32, (LANES, SPAN), 0)
    contract = (((1,), (1,)), ((), ()))

    def one(step, carry):
        entry = entry_ref[step]
        row = row_ref[entry]
        shift = shift_ref[entry]
        skip, fine = shift // LANES, shift % LANES
        for tile in range(blocks + KW - 1):
            line_ref[tile : tile + 1, :] = series_ref[skip + tile, pl.ds(row, 1), :]
        lines = line_ref[...]
        squares = lines * lines
        high = squares.astype(jnp.bfloat16).astype(jnp.float32)
        high_ref[...] = high
        low_ref[...] = squares - high
        def windows(ref):
            return jnp.concatenate(
                [ref[k : k + blocks, :].astype(jnp.bfloat16) for k in range(KW)], axis=1
            )

        wave = wave_ref[pl.ds(entry, 1), :]
        power = jnp.sum(wave * wave, axis=1, keepdims=True)
        base = pltpu.roll(jnp.broadcast_to(wave, (8, SPAN)), fine, 1)
        banded = pltpu.roll(
            jnp.concatenate([base] * (LANES // 8), axis=0), 0, 1, stride=1, stride_axis=0
        ).astype(jnp.bfloat16)
        inside = (lag >= fine) & (lag < fine + length)
        mask = jnp.where(inside, 1.0, 0.0).astype(jnp.bfloat16)
        product = lax.dot_general(windows(line_ref), banded, contract, preferred_element_type=jnp.float32)
        energy = lax.dot_general(
            windows(high_ref), mask, contract, preferred_element_type=jnp.float32
        ) + lax.dot_general(windows(low_ref), mask, contract, preferred_element_type=jnp.float32)
        scale = (energy / length + EPSILON) * (power / length + EPSILON)
        normalized = product / length / jnp.sqrt(scale)
        template = entry // channels
        for block in range(blocks):
            at = (place_of(block, bits) ^ my_place, pl.ds(template, 1), slice(None))
            out_ref[at] = out_ref[at] + normalized[block : block + 1, :]
        return carry

    lax.fori_loop(0, count_ref[0], one, 0)


VMEM_SPEC = pl.BlockSpec(memory_space=pltpu.VMEM)
SMEM_SPEC = pl.BlockSpec(memory_space=pltpu.SMEM)


def kernel_call(body, scalars, arrays, outs, scratch, flops, moved):
    return pl.pallas_call(
        body,
        out_shape=outs,
        in_specs=[SMEM_SPEC] * len(scalars) + [VMEM_SPEC] * len(arrays),
        out_specs=jax.tree.map(lambda _: VMEM_SPEC, outs),
        scratch_shapes=scratch,
        compiler_params=pltpu.CompilerParams(vmem_limit_bytes=VMEM_LIMIT),
        cost_estimate=pl.CostEstimate(flops=flops, bytes_accessed=moved, transcendentals=0),
    )(*scalars, *arrays)


def reduce_stack(partial, bits):
    count = partial.shape[0]
    for bit in bits:
        half = partial.shape[0] // 2
        pairs = [(i, i ^ (1 << bit)) for i in range(count)]
        partial = partial[:half] + lax.ppermute(partial[half:], "stn", pairs)
    return partial[0]


def owned_entries(slots, template_channels):
    flat = template_channels.reshape(-1)
    count = flat.shape[0]
    match = (flat[None, :] == slots[:, None]).astype(jnp.int32)
    row = jnp.sum(match * jnp.arange(slots.shape[0], dtype=jnp.int32)[:, None], axis=0)
    here = jnp.sum(match, axis=0)
    number = jnp.arange(count, dtype=jnp.int32)
    before = jnp.sum(jnp.where(number[None, :] < number[:, None], here[None, :], 0), axis=1)
    where_to = jnp.where(here > 0, before, count)
    entries = jnp.sum(jnp.where(where_to[None, :] == number[:, None], number[None, :], 0), axis=1)
    return entries, row, jnp.sum(here).reshape(1)


def rank_among(slots, rows):
    target = slots // rows
    number = jnp.arange(rows, dtype=jnp.int32)
    same = (target[..., :, None] == target[..., None, :]) & (number[None, :] < number[:, None])
    return target, jnp.sum(same.astype(jnp.int32), axis=-1)


def shards(archive, slot_of_row, templates, template_channels, moveouts, *, sizes):
    stations = lax.axis_size("stn")
    my_index = lax.axis_index("stn")
    which = lax.axis_index("tpl").astype(jnp.int32)
    rows, samples = archive.shape
    half = rows // 2
    local_templates, channels, length = templates.shape
    tiles = stations // 2
    tail_tiles = (samples // LANES - 2 * tiles) // 2
    block_lines = half + 2 * tail_tiles + 8
    f32, bf16, i32 = jnp.float32, jnp.bfloat16, jnp.int32
    shape = jax.ShapeDtypeStruct

    target, rank = rank_among(slot_of_row, rows)
    info = jnp.concatenate([target, slot_of_row % rows + rows * rank]).astype(f32)
    info = jnp.broadcast_to(info[None, :], (8, LANES))
    packed = kernel_call(
        functools.partial(pack_kernel, rows=rows, tiles=tiles, tail_tiles=tail_tiles),
        (which.reshape(1), target * 2 + rank),
        (info, archive),
        shape((stations, block_lines, LANES), bf16),
        [pltpu.VMEM((stations * 2 * tail_tiles, LANES), f32)],
        4_000_000, 4_000_000,
    )
    packed, later_archive = lax.optimization_barrier((packed, archive))
    first = lax.all_to_all(packed, "stn", 0, 0, tiled=True)

    entries, entry_row, entry_count = owned_entries(slot_of_row, template_channels)
    waves = jnp.pad(templates.reshape(-1, length).astype(f32), ((0, 0), (0, SPAN - length)))
    padded = samples // LANES + 8
    bits = halving_bits(sizes)
    my_place = place_of(my_index.astype(i32), bits).reshape(1)
    partial = kernel_call(
        functools.partial(correlate_kernel, length=length, channels=channels, bits=bits),
        (entry_count, entries, entry_row, moveouts.reshape(-1), my_place),
        (later_archive, waves),
        shape((stations, local_templates, LANES), f32),
        [
            pltpu.VMEM((padded, rows, LANES), f32),
            pltpu.VMEM((LANES + 8, LANES), f32),
            pltpu.VMEM((LANES + 8, LANES), f32),
            pltpu.VMEM((LANES + 8, LANES), f32),
        ],
        1000, 1000,
    )
    stack = reduce_stack(partial, bits) * math.sqrt(length / channels)

    lines, tail_rows = kernel_call(
        functools.partial(permute_kernel, rows=rows, tail_tiles=tail_tiles),
        (my_index.astype(i32).reshape(1),),
        (first,),
        (shape((2 * stations, half, LANES), bf16), shape((rows, tail_tiles * LANES), bf16)),
        [
            pltpu.VMEM((2 * stations * half, LANES), f32),
            pltpu.VMEM((stations * rows, LANES), f32),
            pltpu.VMEM((stations * 2 * tail_tiles, LANES), f32),
            pltpu.VMEM((tail_tiles, rows + 8, LANES), f32),
            pltpu.VMEM((stations, LANES), f32),
            pltpu.VMEM((stations, LANES), i32),
            pltpu.VMEM((stations, LANES), i32),
            pltpu.SMEM((stations, LANES), i32),
            pltpu.SMEM((stations, LANES), i32),
            pltpu.SemaphoreType.DMA,
            pltpu.SemaphoreType.DMA,
        ],
        4_000_000, 8_000_000,
    )
    second = lax.all_to_all(lines, ("stn", "tpl"), 0, 0, tiled=True)
    tail_other = lax.ppermute(tail_rows, "tpl", [(0, 1), (1, 0)])
    tail_low = jnp.where(which == 0, tail_rows, tail_other)
    tail_high = jnp.where(which == 0, tail_other, tail_rows)
    grouped = kernel_call(
        functools.partial(assemble_kernel, tiles=tiles),
        (),
        (second, tail_low, tail_high),
        shape((rows, samples), bf16),
        [],
        4_000_000, 6_000_000,
    )
    return grouped, stack


def solution(mesh):
    sizes = (2, 8, 4, 2)
    in_specs = (P("stn", None), P("stn"), P("tpl", None, None), P("tpl", None), P("tpl", None))
    out_specs = (P("stn", None), P("tpl", "stn"))
    return jax.shard_map(
        functools.partial(shards, sizes=sizes), mesh=mesh, in_specs=in_specs, out_specs=out_specs, check_vma=False
    )
```

```python
import functools
import math

import jax
import jax.numpy as jnp
from jax import lax
from jax.experimental import pallas as pl
from jax.experimental.pallas import tpu as pltpu
from jax.sharding import PartitionSpec as P

EPSILON = 1e-06
LANES = 128
KW = 7
SPAN = KW * LANES
MIB = 1024 * 1024
PARTS = 4


def roll_half(x):
    return pltpu.roll(x, LANES // 2, 1)


def left_lanes(rows):
    return lax.broadcasted_iota(jnp.int32, (rows, LANES), 1) < LANES // 2


def send_part(source, target, part, size, sem):
    at = pl.ds(part * size, size)
    copy = pltpu.make_async_copy(source.at[at], target.at[at], sem)
    copy.start()
    return copy


def pack_kernel(
    half_ref, base_ref, info_ref, archive_ref, out_hbm, out_ref, tail_ref, sems, *, rows, tiles, tail_tiles
):
    which = half_ref[0]
    half = rows // 2
    left = left_lanes(half)
    owners = out_ref.shape[0]
    tail_lines = 2 * tail_tiles
    tail_ref[...] = jnp.zeros_like(tail_ref)
    tail_start = 2 * tiles * LANES
    info = info_ref[...]
    for tile in range(tail_tiles):
        at = pl.multiple_of(tail_start + (which * tail_tiles + tile) * LANES, LANES)
        block = archive_ref[:, pl.ds(at, LANES)].astype(jnp.float32)
        for row in range(rows):
            tail_ref[pl.ds(base_ref[row] * tail_tiles + tile, 1), :] = block[row : row + 1, :]

    def one(tile, carry):
        at = pl.multiple_of((which * tiles + tile) * LANES, LANES)
        block = archive_ref[:, pl.ds(at, LANES)].astype(jnp.float32)
        upper, lower = block[:half], block[half:]
        even = jnp.where(left, upper, roll_half(lower))
        odd = jnp.where(left, roll_half(upper), lower)
        for side, lines in ((0, even), (1, odd)):
            owner = 2 * tile + side
            tail = tail_ref[pl.ds(pl.multiple_of(owner * tail_lines, 8), tail_lines), :]
            out_ref[owner] = jnp.concatenate([lines, tail, info], axis=0).astype(jnp.bfloat16)
        return carry

    copies = []
    for part in range(PARTS):
        lax.fori_loop(part * tiles // PARTS, (part + 1) * tiles // PARTS, one, 0, unroll=8)
        copies.append(send_part(out_ref, out_hbm, part, owners // PARTS, sems.at[part]))
    for copy in copies:
        copy.wait()


def permute_kernel(
    owner_ref, got_ref, out_hbm, tail_out_ref,
    out_ref, plain_ref, placed_ref, tail_ref, tail_rows_ref, info_ref, route_ref, route_smem, route_sem, sems,
    *, rows, tail_tiles,
):
    stations = got_ref.shape[0]
    half = rows // 2
    left = left_lanes(half)
    tail_lines = 2 * tail_tiles

    def note(station, carry):
        info_ref[pl.ds(station, 1), :] = got_ref[station][half + tail_lines : half + tail_lines + 8].astype(
            jnp.float32
        )[:1]
        return carry

    lax.fori_loop(0, stations, note, 0, unroll=8)
    info = info_ref[...].astype(jnp.int32)
    other = pltpu.roll(info_ref[...], rows, 1).astype(jnp.int32)
    on_left = lax.broadcasted_iota(jnp.int32, info.shape, 1) < rows
    target = jnp.where(on_left, info, other)
    packed = jnp.where(on_left, other, info)
    place, rank = packed % rows, packed // rows
    mine = target == owner_ref[0]
    first = jnp.max(jnp.where(mine & (rank == 0), place, -1), axis=1, keepdims=True)
    second = jnp.max(jnp.where(mine & (rank == 1), place, -1), axis=1, keepdims=True)
    lane = lax.broadcasted_iota(jnp.int32, info.shape, 1)
    kept = jnp.where(lane == rows, first, second)
    kept = jnp.where(kept < 0, rows, kept)
    route_ref[...] = jnp.where(on_left, target * rows + place, kept)
    route_copy = pltpu.make_async_copy(route_ref, route_smem, route_sem)
    route_copy.start()

    def expand(station, carry):
        block = got_ref[station].astype(jnp.float32)
        lines = block[:half]
        at = pl.multiple_of(station * rows, 8)
        plain_ref[pl.ds(at, half), :] = lines
        plain_ref[pl.ds(at + half, half), :] = roll_half(lines)
        tail_ref[pl.ds(pl.multiple_of(station * tail_lines, 8), tail_lines), :] = block[half : half + tail_lines]
        return carry

    lax.fori_loop(0, stations, expand, 0, unroll=8)
    route_copy.wait()

    def move(station, carry):
        lines = plain_ref[pl.ds(pl.multiple_of(station * rows, 8), rows), :]
        for row in range(rows):
            placed_ref[pl.ds(route_smem[station, row], 1), :] = lines[row : row + 1, :]
        return carry

    lax.fori_loop(0, stations, move, 0)

    def join(station, carry):
        at = pl.multiple_of(station * rows, 8)
        lines = jnp.where(left, placed_ref[pl.ds(at, half), :], roll_half(placed_ref[pl.ds(at + half, half), :]))
        out_ref[station] = lines.astype(jnp.bfloat16)
        return carry

    copies = []
    for part in range(PARTS):
        lax.fori_loop(part * stations // PARTS, (part + 1) * stations // PARTS, join, 0, unroll=8)
        for which in range(2):
            copies.append(
                send_part(out_ref, out_hbm.at[:, which], part, stations // PARTS, sems.at[which, part])
            )
    def keep(station, carry):
        for rank in range(2):
            row = route_smem[station, rows + rank]
            for tile in range(tail_tiles):
                line = station * tail_lines + rank * tail_tiles + tile
                tail_rows_ref[tile, pl.ds(row, 1), :] = tail_ref[pl.ds(line, 1), :]
        return carry

    lax.fori_loop(0, stations, keep, 0, unroll=8)
    for tile in range(tail_tiles):
        tail_out_ref[:, tile * LANES : (tile + 1) * LANES] = tail_rows_ref[tile, :rows, :].astype(jnp.bfloat16)
    for copy in copies:
        copy.wait()


def assemble_kernel(got_ref, tail_low_ref, tail_high_ref, out_hbm, out_ref, sems, *, tiles):
    half = got_ref.shape[1]
    left = left_lanes(half)
    copies = []

    def send(start, size):
        at = (slice(None), pl.ds(start, size))
        copies.append(pltpu.make_async_copy(out_ref.at[at], out_hbm.at[at], sems.at[len(copies)]))
        copies[-1].start()

    at = 2 * tiles * LANES
    width = tail_low_ref.shape[1]
    out_ref[:, at : at + width] = tail_low_ref[...]
    out_ref[:, at + width : at + 2 * width] = tail_high_ref[...]
    send(at, 2 * width)
    for which in range(2):

        def one(tile, carry, which=which):
            even = got_ref[4 * tile + which].astype(jnp.float32)
            odd = got_ref[4 * tile + 2 + which].astype(jnp.float32)
            upper = jnp.where(left, even, roll_half(odd))
            lower = jnp.where(left, roll_half(even), odd)
            at = pl.multiple_of((which * tiles + tile) * LANES, LANES)
            out_ref[:, pl.ds(at, LANES)] = jnp.concatenate([upper, lower], axis=0).astype(jnp.bfloat16)
            return carry

        part = tiles // 2
        for start in range(0, tiles, part):
            lax.fori_loop(start, start + part, one, 0, unroll=8)
            send((which * tiles + start) * LANES, part * LANES)
    for copy in copies:
        copy.wait()


def halving_bits(sizes):
    ys, zs, xs, cores = (size.bit_length() - 1 for size in sizes)
    x_from, z_from, y_from = cores, cores + xs, cores + xs + zs
    return (
        list(range(cores))
        + list(range(y_from, y_from + ys))
        + list(range(x_from, z_from))
        + list(reversed(range(z_from, y_from)))
    )


def place_of(index, bits):
    place = 0
    for at, bit in enumerate(bits):
        place = place + ((index >> bit) & 1) * (1 << (len(bits) - 1 - at))
    return place


def correlate_kernel(
    count_ref, entry_ref, row_ref, shift_ref, place_ref, archive_ref, wave_ref, out_ref,
    series_ref, line_ref, high_ref, low_ref, *, length, channels, bits,
):
    rows = archive_ref.shape[0]
    tiles = archive_ref.shape[1] // LANES
    blocks = LANES
    padded = series_ref.shape[0]

    def widen(tile, carry):
        at = pl.multiple_of(tile * LANES, LANES)
        series_ref[tile] = archive_ref[:, pl.ds(at, LANES)].astype(jnp.float32)
        return carry

    lax.fori_loop(0, tiles, widen, 0, unroll=8)
    for tile in range(tiles, padded):
        series_ref[tile] = jnp.zeros((rows, LANES), jnp.float32)
    out_ref[...] = jnp.zeros_like(out_ref)
    line_ref[...] = jnp.zeros_like(line_ref)
    my_place = place_ref[0]
    lag = lax.broadcasted_iota(jnp.int32, (LANES, SPAN), 1) - lax.broadcasted_iota(jnp.int32, (LANES, SPAN), 0)
    contract = (((1,), (1,)), ((), ()))

    def one(step, carry):
        entry = entry_ref[step]
        row = row_ref[entry]
        shift = shift_ref[entry]
        skip, fine = shift // LANES, shift % LANES
        for tile in range(blocks + KW - 1):
            line_ref[tile : tile + 1, :] = series_ref[skip + tile, pl.ds(row, 1), :]
        lines = line_ref[...]
        squares = lines * lines
        high = squares.astype(jnp.bfloat16).astype(jnp.float32)
        high_ref[...] = high
        low_ref[...] = squares - high
        def windows(ref):
            return jnp.concatenate(
                [ref[k : k + blocks, :].astype(jnp.bfloat16) for k in range(KW)], axis=1
            )

        wave = wave_ref[pl.ds(entry, 1), :]
        power = jnp.sum(wave * wave, axis=1, keepdims=True)
        base = pltpu.roll(jnp.broadcast_to(wave, (8, SPAN)), fine, 1)
        banded = pltpu.roll(
            jnp.concatenate([base] * (LANES // 8), axis=0), 0, 1, stride=1, stride_axis=0
        ).astype(jnp.bfloat16)
        inside = (lag >= fine) & (lag < fine + length)
        mask = jnp.where(inside, 1.0, 0.0).astype(jnp.bfloat16)
        product = lax.dot_general(windows(line_ref), banded, contract, preferred_element_type=jnp.float32)
        energy = lax.dot_general(
            windows(high_ref), mask, contract, preferred_element_type=jnp.float32
        ) + lax.dot_general(windows(low_ref), mask, contract, preferred_element_type=jnp.float32)
        scale = (energy / length + EPSILON) * (power / length + EPSILON)
        normalized = product / length / jnp.sqrt(scale)
        template = entry // channels
        for block in range(blocks):
            at = (place_of(block, bits) ^ my_place, pl.ds(template, 1), slice(None))
            out_ref[at] = out_ref[at] + normalized[block : block + 1, :]
        return carry

    lax.fori_loop(0, count_ref[0], one, 0)


VMEM_SPEC = pl.BlockSpec(memory_space=pltpu.VMEM)
SMEM_SPEC = pl.BlockSpec(memory_space=pltpu.SMEM)
HBM_SPEC = pl.BlockSpec(memory_space=pltpu.HBM)


def kernel_call(body, scalars, arrays, outs, scratch, flops, moved, vmem, out_specs=VMEM_SPEC):
    return pl.pallas_call(
        body,
        out_shape=outs,
        in_specs=[SMEM_SPEC] * len(scalars) + [VMEM_SPEC] * len(arrays),
        out_specs=out_specs,
        scratch_shapes=scratch,
        compiler_params=pltpu.CompilerParams(vmem_limit_bytes=vmem * MIB),
        cost_estimate=pl.CostEstimate(flops=flops, bytes_accessed=moved, transcendentals=0),
    )(*scalars, *arrays)


def halve(partial, bit, count):
    half = partial.shape[0] // 2
    pairs = [(i, i ^ (1 << bit)) for i in range(count)]
    return partial[:half] + lax.ppermute(partial[half:], "stn", pairs)


def owned_entries(slots, template_channels):
    flat = template_channels.reshape(-1)
    count = flat.shape[0]
    match = (flat[None, :] == slots[:, None]).astype(jnp.int32)
    row = jnp.sum(match * jnp.arange(slots.shape[0], dtype=jnp.int32)[:, None], axis=0)
    here = jnp.sum(match, axis=0)
    number = jnp.arange(count, dtype=jnp.int32)
    before = jnp.sum(jnp.where(number[None, :] < number[:, None], here[None, :], 0), axis=1)
    where_to = jnp.where(here > 0, before, count)
    entries = jnp.sum(jnp.where(where_to[None, :] == number[:, None], number[None, :], 0), axis=1)
    return entries, row, jnp.sum(here).reshape(1)


def rank_among(slots, rows):
    target = slots // rows
    number = jnp.arange(rows, dtype=jnp.int32)
    same = (target[..., :, None] == target[..., None, :]) & (number[None, :] < number[:, None])
    return target, jnp.sum(same.astype(jnp.int32), axis=-1)


def shards(archive, slot_of_row, templates, template_channels, moveouts, *, sizes):
    stations = lax.axis_size("stn")
    my_index = lax.axis_index("stn")
    which = lax.axis_index("tpl").astype(jnp.int32)
    rows, samples = archive.shape
    half = rows // 2
    local_templates, channels, length = templates.shape
    tiles = stations // 2
    tail_tiles = (samples // LANES - 2 * tiles) // 2
    block_lines = half + 2 * tail_tiles + 8
    f32, bf16, i32 = jnp.float32, jnp.bfloat16, jnp.int32
    shape = jax.ShapeDtypeStruct

    target, rank = rank_among(slot_of_row, rows)
    info = jnp.concatenate([target, slot_of_row % rows + rows * rank]).astype(f32)
    info = jnp.broadcast_to(info[None, :], (8, LANES))
    packed = kernel_call(
        functools.partial(pack_kernel, rows=rows, tiles=tiles, tail_tiles=tail_tiles),
        (which.reshape(1), target * 2 + rank),
        (info, archive),
        shape((stations, block_lines, LANES), bf16),
        [
            pltpu.VMEM((stations, block_lines, LANES), bf16),
            pltpu.VMEM((stations * 2 * tail_tiles, LANES), f32),
            pltpu.SemaphoreType.DMA((PARTS,)),
        ],
        4_000_000, 4_000_000, 12, HBM_SPEC,
    )
    packed, later_archive = lax.optimization_barrier((packed, archive))
    first = lax.all_to_all(packed, "stn", 0, 0, tiled=True)

    entries, entry_row, entry_count = owned_entries(slot_of_row, template_channels)
    waves = jnp.pad(templates.reshape(-1, length).astype(f32), ((0, 0), (0, SPAN - length)))
    padded = samples // LANES + 8
    bits = halving_bits(sizes)
    my_place = place_of(my_index.astype(i32), bits).reshape(1)
    partial = kernel_call(
        functools.partial(correlate_kernel, length=length, channels=channels, bits=bits),
        (entry_count, entries, entry_row, moveouts.reshape(-1), my_place),
        (later_archive, waves),
        shape((stations, local_templates, LANES), f32),
        [
            pltpu.VMEM((padded, rows, LANES), f32),
            pltpu.VMEM((LANES + 8, LANES), f32),
            pltpu.VMEM((LANES + 8, LANES), f32),
            pltpu.VMEM((LANES + 8, LANES), f32),
        ],
        1000, 1000, 28,
    )
    partial = halve(partial, bits[0], stations)
    first, _ = lax.optimization_barrier((first, partial))
    for bit in bits[1:]:
        partial = halve(partial, bit, stations)
    stack = partial[0] * math.sqrt(length / channels)

    lines, tail_rows = kernel_call(
        functools.partial(permute_kernel, rows=rows, tail_tiles=tail_tiles),
        (my_index.astype(i32).reshape(1),),
        (first,),
        (shape((stations, 2, half, LANES), bf16), shape((rows, tail_tiles * LANES), bf16)),
        [
            pltpu.VMEM((stations, half, LANES), bf16),
            pltpu.VMEM((stations * rows, LANES), f32),
            pltpu.VMEM((stations * rows, LANES), f32),
            pltpu.VMEM((stations * 2 * tail_tiles, LANES), f32),
            pltpu.VMEM((tail_tiles, rows + 8, LANES), f32),
            pltpu.VMEM((stations, LANES), f32),
            pltpu.VMEM((stations, LANES), i32),
            pltpu.SMEM((stations, LANES), i32),
            pltpu.SemaphoreType.DMA,
            pltpu.SemaphoreType.DMA((2, PARTS)),
        ],
        4_000_000, 30_000_000, 52, (HBM_SPEC, VMEM_SPEC),
    )
    lines = lines.reshape(2 * stations, half, LANES)
    second = lax.all_to_all(lines, ("stn", "tpl"), 0, 0, tiled=True)
    tail_other = lax.ppermute(tail_rows, "tpl", [(0, 1), (1, 0)])
    tail_low = jnp.where(which == 0, tail_rows, tail_other)
    tail_high = jnp.where(which == 0, tail_other, tail_rows)
    grouped = kernel_call(
        functools.partial(assemble_kernel, tiles=tiles),
        (),
        (second, tail_low, tail_high),
        shape((rows, samples), bf16),
        [pltpu.VMEM((rows, samples), bf16), pltpu.SemaphoreType.DMA((5,))],
        4_000_000, 6_000_000, 12, HBM_SPEC,
    )
    return grouped, stack


def solution(mesh):
    sizes = (2, 8, 4, 2)
    in_specs = (P("stn", None), P("stn"), P("tpl", None, None), P("tpl", None), P("tpl", None))
    out_specs = (P("stn", None), P("tpl", "stn"))
    return jax.shard_map(
        functools.partial(shards, sizes=sizes), mesh=mesh, in_specs=in_specs, out_specs=out_specs, check_vma=False
    )
```

```python
import functools
import math

import jax
import jax.numpy as jnp
from jax import lax
from jax.experimental import pallas as pl
from jax.experimental.pallas import tpu as pltpu
from jax.sharding import PartitionSpec as P

EPSILON = 1e-06
LANES = 128
KW = 7
SPAN = KW * LANES
MIB = 1024 * 1024
PARTS = 4
GROUP = 16
EARLY = 3


def roll_half(x):
    return pltpu.roll(x, LANES // 2, 1)


def left_lanes(rows):
    return lax.broadcasted_iota(jnp.int32, (rows, LANES), 1) < LANES // 2


def send_part(source, target, part, size, sem):
    at = pl.ds(part * size, size)
    copy = pltpu.make_async_copy(source.at[at], target.at[at], sem)
    copy.start()
    return copy


def pack_kernel(
    half_ref, base_ref, info_ref, archive_hbm, out_hbm, archive_ref, out_ref, tail_ref, get_sems, sems,
    *, rows, tiles, tail_tiles,
):
    which = half_ref[0]
    half = rows // 2
    left = left_lanes(half)
    owners = out_ref.shape[0]
    tail_lines = 2 * tail_tiles
    width, tail_width = tiles * LANES, tail_tiles * LANES

    def fetch(start, at, size, number):
        start = pl.multiple_of(start, LANES)
        copy = pltpu.make_async_copy(
            archive_hbm.at[:, pl.ds(start, size)], archive_ref.at[:, pl.ds(at, size)], get_sems.at[number]
        )
        copy.start()
        return copy

    tail_fetch = fetch(2 * width + which * tail_width, width, tail_width, PARTS)
    part_width = width // PARTS
    fetches = [fetch(which * width + part * part_width, part * part_width, part_width, part) for part in range(PARTS)]
    tail_ref[...] = jnp.zeros_like(tail_ref)
    info = info_ref[...]
    tail_fetch.wait()
    for tile in range(tail_tiles):
        at = width + tile * LANES
        block = archive_ref[:, at : at + LANES].astype(jnp.float32)
        for row in range(rows):
            tail_ref[pl.ds(base_ref[row] * tail_tiles + tile, 1), :] = block[row : row + 1, :]

    def one(tile, carry):
        at = pl.multiple_of(tile * LANES, LANES)
        block = archive_ref[:, pl.ds(at, LANES)].astype(jnp.float32)
        upper, lower = block[:half], block[half:]
        even = jnp.where(left, upper, roll_half(lower))
        odd = jnp.where(left, roll_half(upper), lower)
        for side, lines in ((0, even), (1, odd)):
            owner = 2 * tile + side
            tail = tail_ref[pl.ds(pl.multiple_of(owner * tail_lines, 8), tail_lines), :]
            out_ref[owner] = jnp.concatenate([lines, tail, info], axis=0).astype(jnp.bfloat16)
        return carry

    copies = []
    for part in range(PARTS):
        fetches[part].wait()
        lax.fori_loop(part * tiles // PARTS, (part + 1) * tiles // PARTS, one, 0, unroll=8)
        copies.append(send_part(out_ref, out_hbm, part, owners // PARTS, sems.at[part]))
    for copy in copies:
        copy.wait()


def permute_kernel(
    owner_ref, got_ref, out_hbm, tail_out_ref,
    out_ref, placed_ref, tail_ref, tail_rows_ref, info_ref, route_ref, route_smem, route_sem, sems,
    *, rows, tail_tiles,
):
    stations = got_ref.shape[0]
    half = rows // 2
    left = left_lanes(half)
    tail_lines = 2 * tail_tiles

    def note(station, carry):
        info_ref[pl.ds(station, 1), :] = got_ref[station][half + tail_lines : half + tail_lines + 8].astype(
            jnp.float32
        )[:1]
        return carry

    lax.fori_loop(0, stations, note, 0, unroll=8)
    info = info_ref[...].astype(jnp.int32)
    other = pltpu.roll(info_ref[...], rows, 1).astype(jnp.int32)
    on_left = lax.broadcasted_iota(jnp.int32, info.shape, 1) < rows
    target = jnp.where(on_left, info, other)
    packed = jnp.where(on_left, other, info)
    place, rank = packed % rows, packed // rows
    mine = target == owner_ref[0]
    first = jnp.max(jnp.where(mine & (rank == 0), place, -1), axis=1, keepdims=True)
    second = jnp.max(jnp.where(mine & (rank == 1), place, -1), axis=1, keepdims=True)
    lane = lax.broadcasted_iota(jnp.int32, info.shape, 1)
    kept = jnp.where(lane == rows, first, second)
    kept = jnp.where(kept < 0, rows, kept)
    route_ref[...] = jnp.where(on_left, target * rows + place, kept)
    route_copy = pltpu.make_async_copy(route_ref, route_smem, route_sem)
    route_copy.start()

    def tails(station, carry):
        block = got_ref[station].astype(jnp.float32)
        tail_ref[pl.ds(pl.multiple_of(station * tail_lines, 8), tail_lines), :] = block[half : half + tail_lines]
        return carry

    lax.fori_loop(0, stations, tails, 0, unroll=8)
    route_copy.wait()

    def move(station, carry):
        upper = got_ref[station].astype(jnp.float32)[:half]
        lower = roll_half(upper)
        for row in range(half):
            placed_ref[pl.ds(route_smem[station, row], 1), :] = upper[row : row + 1, :]
        for row in range(half):
            placed_ref[pl.ds(route_smem[station, half + row], 1), :] = lower[row : row + 1, :]
        return carry

    lax.fori_loop(0, stations, move, 0, unroll=2)

    def join(station, carry):
        at = pl.multiple_of(station * rows, 8)
        lines = jnp.where(left, placed_ref[pl.ds(at, half), :], roll_half(placed_ref[pl.ds(at + half, half), :]))
        out_ref[station] = lines.astype(jnp.bfloat16)
        return carry

    copies = []
    for part in range(PARTS):
        lax.fori_loop(part * stations // PARTS, (part + 1) * stations // PARTS, join, 0, unroll=8)
        for which in range(2):
            copies.append(
                send_part(out_ref, out_hbm.at[:, which], part, stations // PARTS, sems.at[which, part])
            )
    def keep(station, carry):
        for rank in range(2):
            row = route_smem[station, rows + rank]
            for tile in range(tail_tiles):
                line = station * tail_lines + rank * tail_tiles + tile
                tail_rows_ref[tile, pl.ds(row, 1), :] = tail_ref[pl.ds(line, 1), :]
        return carry

    lax.fori_loop(0, stations, keep, 0, unroll=8)
    for tile in range(tail_tiles):
        tail_out_ref[:, tile * LANES : (tile + 1) * LANES] = tail_rows_ref[tile, :rows, :].astype(jnp.bfloat16)
    for copy in copies:
        copy.wait()


def assemble_kernel(got_ref, tail_low_ref, tail_high_ref, out_hbm, out_ref, sems, *, tiles):
    half = got_ref.shape[1]
    left = left_lanes(half)
    copies = []

    def send(start, size):
        at = (slice(None), pl.ds(start, size))
        copies.append(pltpu.make_async_copy(out_ref.at[at], out_hbm.at[at], sems.at[len(copies)]))
        copies[-1].start()

    at = 2 * tiles * LANES
    width = tail_low_ref.shape[1]
    out_ref[:, at : at + width] = tail_low_ref[...]
    out_ref[:, at + width : at + 2 * width] = tail_high_ref[...]
    send(at, 2 * width)
    for which in range(2):

        def one(tile, carry, which=which):
            even = got_ref[4 * tile + which].astype(jnp.float32)
            odd = got_ref[4 * tile + 2 + which].astype(jnp.float32)
            upper = jnp.where(left, even, roll_half(odd))
            lower = jnp.where(left, roll_half(even), odd)
            at = pl.multiple_of((which * tiles + tile) * LANES, LANES)
            out_ref[:, pl.ds(at, LANES)] = jnp.concatenate([upper, lower], axis=0).astype(jnp.bfloat16)
            return carry

        part = tiles // 2
        for start in range(0, tiles, part):
            lax.fori_loop(start, start + part, one, 0, unroll=8)
            send((which * tiles + start) * LANES, part * LANES)
    for copy in copies:
        copy.wait()


def halving_bits(sizes):
    ys, zs, xs, cores = (size.bit_length() - 1 for size in sizes)
    x_from, z_from, y_from = cores, cores + xs, cores + xs + zs
    return (
        list(range(cores))
        + list(range(y_from, y_from + ys))
        + list(range(x_from, z_from))
        + list(reversed(range(z_from, y_from)))
    )


def place_of(index, bits):
    place = 0
    for at, bit in enumerate(bits):
        place = place + ((index >> bit) & 1) * (1 << (len(bits) - 1 - at))
    return place


def correlate_kernel(
    count_ref, entry_ref, row_ref, shift_ref, place_ref, archive_ref, wave_ref, out_ref,
    series_ref, line_ref, high_ref, low_ref, group_ref, *, length, bits,
):
    rows = archive_ref.shape[0]
    tiles = archive_ref.shape[1] // LANES
    blocks = LANES
    padded = series_ref.shape[0]

    def widen(tile, carry):
        at = pl.multiple_of(tile * LANES, LANES)
        series_ref[tile] = archive_ref[:, pl.ds(at, LANES)].astype(jnp.float32)
        return carry

    lax.fori_loop(0, tiles, widen, 0, unroll=8)
    for tile in range(tiles, padded):
        series_ref[tile] = jnp.zeros((rows, LANES), jnp.float32)
    out_ref[...] = jnp.zeros_like(out_ref)
    line_ref[...] = jnp.zeros_like(line_ref)
    my_place = place_ref[0]
    lag = lax.broadcasted_iota(jnp.int32, (LANES, SPAN), 1) - lax.broadcasted_iota(jnp.int32, (LANES, SPAN), 0)
    contract = (((1,), (1,)), ((), ()))

    def one(step, carry):
        entry = entry_ref[step]
        row = row_ref[entry]
        shift = shift_ref[entry]
        skip, fine = shift // LANES, shift % LANES
        for tile in range(blocks + KW - 1):
            line_ref[tile : tile + 1, :] = series_ref[skip + tile, pl.ds(row, 1), :]
        lines = line_ref[...]
        squares = lines * lines
        high = squares.astype(jnp.bfloat16).astype(jnp.float32)
        high_ref[...] = high
        low_ref[...] = squares - high
        def windows(ref):
            return jnp.concatenate(
                [ref[k : k + blocks, :].astype(jnp.bfloat16) for k in range(KW)], axis=1
            )

        group = pl.multiple_of(entry // GROUP * GROUP, GROUP)
        group_ref[...] = wave_ref[pl.ds(group, GROUP), :].astype(jnp.float32)
        wave = jnp.concatenate(
            [group_ref[pl.ds(entry % GROUP, 1), :], jnp.zeros((1, SPAN - length), jnp.float32)], axis=1
        )
        power = jnp.sum(wave * wave, axis=1, keepdims=True)
        base = pltpu.roll(jnp.broadcast_to(wave, (8, SPAN)), fine, 1)
        banded = pltpu.roll(
            jnp.concatenate([base] * (LANES // 8), axis=0), 0, 1, stride=1, stride_axis=0
        ).astype(jnp.bfloat16)
        inside = (lag >= fine) & (lag < fine + length)
        mask = jnp.where(inside, 1.0, 0.0).astype(jnp.bfloat16)
        product = lax.dot_general(windows(line_ref), banded, contract, preferred_element_type=jnp.float32)
        energy = lax.dot_general(
            windows(high_ref), mask, contract, preferred_element_type=jnp.float32
        ) + lax.dot_general(windows(low_ref), mask, contract, preferred_element_type=jnp.float32)
        scale = (energy / length + EPSILON) * (power / length + EPSILON)
        normalized = product / length / jnp.sqrt(scale)
        template = entry % out_ref.shape[1]
        for block in range(blocks):
            at = (place_of(block, bits) ^ my_place, pl.ds(template, 1), slice(None))
            out_ref[at] = out_ref[at] + normalized[block : block + 1, :]
        return carry

    lax.fori_loop(0, count_ref[0], one, 0)


VMEM_SPEC = pl.BlockSpec(memory_space=pltpu.VMEM)
SMEM_SPEC = pl.BlockSpec(memory_space=pltpu.SMEM)
HBM_SPEC = pl.BlockSpec(memory_space=pltpu.HBM)


def kernel_call(
    body, scalars, arrays, outs, scratch, flops, moved, vmem, out_specs=VMEM_SPEC, in_specs=None
):
    return pl.pallas_call(
        body,
        out_shape=outs,
        in_specs=[SMEM_SPEC] * len(scalars) + (in_specs or [VMEM_SPEC] * len(arrays)),
        out_specs=out_specs,
        scratch_shapes=scratch,
        compiler_params=pltpu.CompilerParams(vmem_limit_bytes=vmem * MIB),
        cost_estimate=pl.CostEstimate(flops=flops, bytes_accessed=moved, transcendentals=0),
    )(*scalars, *arrays)


def halve(partial, bit, count):
    half = partial.shape[0] // 2
    pairs = [(i, i ^ (1 << bit)) for i in range(count)]
    return partial[:half] + lax.ppermute(partial[half:], "stn", pairs)


def owned_entries(slots, template_channels):
    flat = template_channels.reshape(-1)
    count = flat.shape[0]
    match = (flat[None, :] == slots[:, None]).astype(jnp.int32)
    row = jnp.sum(match * jnp.arange(slots.shape[0], dtype=jnp.int32)[:, None], axis=0)
    here = jnp.sum(match, axis=0)
    number = jnp.arange(count, dtype=jnp.int32)
    before = jnp.sum(jnp.where(number[None, :] < number[:, None], here[None, :], 0), axis=1)
    where_to = jnp.where(here > 0, before, count)
    entries = jnp.sum(jnp.where(where_to[None, :] == number[:, None], number[None, :], 0), axis=1)
    return entries, row, jnp.sum(here).reshape(1)


def rank_among(slots, rows):
    target = slots // rows
    number = jnp.arange(rows, dtype=jnp.int32)
    same = (target[..., :, None] == target[..., None, :]) & (number[None, :] < number[:, None])
    return target, jnp.sum(same.astype(jnp.int32), axis=-1)


def shards(archive, slot_of_row, templates, template_channels, moveouts, *, sizes):
    stations = lax.axis_size("stn")
    my_index = lax.axis_index("stn")
    which = lax.axis_index("tpl").astype(jnp.int32)
    rows, samples = archive.shape
    half = rows // 2
    local_templates, channels, length = templates.shape
    tiles = stations // 2
    tail_tiles = (samples // LANES - 2 * tiles) // 2
    block_lines = half + 2 * tail_tiles + 8
    f32, bf16, i32 = jnp.float32, jnp.bfloat16, jnp.int32
    shape = jax.ShapeDtypeStruct

    target, rank = rank_among(slot_of_row, rows)
    info = jnp.concatenate([target, slot_of_row % rows + rows * rank]).astype(f32)
    info = jnp.broadcast_to(info[None, :], (8, LANES))
    packed = kernel_call(
        functools.partial(pack_kernel, rows=rows, tiles=tiles, tail_tiles=tail_tiles),
        (which.reshape(1), target * 2 + rank),
        (info, archive),
        shape((stations, block_lines, LANES), bf16),
        [
            pltpu.VMEM((rows, (tiles + tail_tiles) * LANES), bf16),
            pltpu.VMEM((stations, block_lines, LANES), bf16),
            pltpu.VMEM((stations * 2 * tail_tiles, LANES), f32),
            pltpu.SemaphoreType.DMA((PARTS + 1,)),
            pltpu.SemaphoreType.DMA((PARTS,)),
        ],
        4_000_000, 4_000_000, 56, HBM_SPEC, [VMEM_SPEC, HBM_SPEC],
    )
    packed, later_archive = lax.optimization_barrier((packed, archive))
    first = lax.all_to_all(packed, "stn", 0, 0, tiled=True)

    entries, entry_row, entry_count = owned_entries(slot_of_row, template_channels.T)
    waves = templates.transpose(1, 0, 2).reshape(-1, length)
    padded = samples // LANES + 8
    bits = halving_bits(sizes)
    my_place = place_of(my_index.astype(i32), bits).reshape(1)
    partial = kernel_call(
        functools.partial(correlate_kernel, length=length, bits=bits),
        (entry_count, entries, entry_row, moveouts.T.reshape(-1), my_place),
        (later_archive, waves),
        shape((stations, local_templates, LANES), f32),
        [
            pltpu.VMEM((padded, rows, LANES), f32),
            pltpu.VMEM((LANES + 8, LANES), f32),
            pltpu.VMEM((LANES + 8, LANES), f32),
            pltpu.VMEM((LANES + 8, LANES), f32),
            pltpu.VMEM((GROUP, length), f32),
        ],
        1000, 1000, 28,
    )
    for bit in bits[:EARLY]:
        partial = halve(partial, bit, stations)
    first, _ = lax.optimization_barrier((first, partial))
    for bit in bits[EARLY:]:
        partial = halve(partial, bit, stations)
    stack = partial[0] * math.sqrt(length / channels)

    lines, tail_rows = kernel_call(
        functools.partial(permute_kernel, rows=rows, tail_tiles=tail_tiles),
        (my_index.astype(i32).reshape(1),),
        (first,),
        (shape((stations, 2, half, LANES), bf16), shape((rows, tail_tiles * LANES), bf16)),
        [
            pltpu.VMEM((stations, half, LANES), bf16),
            pltpu.VMEM((stations * rows, LANES), f32),
            pltpu.VMEM((stations * 2 * tail_tiles, LANES), f32),
            pltpu.VMEM((tail_tiles, rows + 8, LANES), f32),
            pltpu.VMEM((stations, LANES), f32),
            pltpu.VMEM((stations, LANES), i32),
            pltpu.SMEM((stations, LANES), i32),
            pltpu.SemaphoreType.DMA,
            pltpu.SemaphoreType.DMA((2, PARTS)),
        ],
        4_000_000, 30_000_000, 52, (HBM_SPEC, VMEM_SPEC),
    )
    lines = lines.reshape(2 * stations, half, LANES)
    second = lax.all_to_all(lines, ("stn", "tpl"), 0, 0, tiled=True)
    tail_other = lax.ppermute(tail_rows, "tpl", [(0, 1), (1, 0)])
    tail_low = jnp.where(which == 0, tail_rows, tail_other)
    tail_high = jnp.where(which == 0, tail_other, tail_rows)
    grouped = kernel_call(
        functools.partial(assemble_kernel, tiles=tiles),
        (),
        (second, tail_low, tail_high),
        shape((rows, samples), bf16),
        [pltpu.VMEM((rows, samples), bf16), pltpu.SemaphoreType.DMA((5,))],
        4_000_000, 6_000_000, 12, HBM_SPEC,
    )
    return grouped, stack


def solution(mesh):
    sizes = (2, 8, 4, 2)
    in_specs = (P("stn", None), P("stn"), P("tpl", None, None), P("tpl", None), P("tpl", None))
    out_specs = (P("stn", None), P("tpl", "stn"))
    return jax.shard_map(
        functools.partial(shards, sizes=sizes), mesh=mesh, in_specs=in_specs, out_specs=out_specs, check_vma=False
    )
```

```python
import functools
import math

import jax
import jax.numpy as jnp
from jax import lax
from jax.experimental import pallas as pl
from jax.experimental.pallas import tpu as pltpu
from jax.sharding import PartitionSpec as P

EPSILON = 1e-06
LANES = 128
KW = 7
SPAN = KW * LANES
MIB = 1024 * 1024
PARTS = 4
GROUP = 16


def roll_half(x):
    return pltpu.roll(x, LANES // 2, 1)


def left_lanes(rows):
    return lax.broadcasted_iota(jnp.int32, (rows, LANES), 1) < LANES // 2


def send_part(source, target, part, size, sem):
    at = pl.ds(part * size, size)
    copy = pltpu.make_async_copy(source.at[at], target.at[at], sem)
    copy.start()
    return copy


def pack_kernel(
    half_ref, slot_ref, archive_hbm, out_hbm, archive_ref, out_ref, tail_ref, base_vmem, base_ref, get_sems, sems, base_sem,
    *, rows, tiles, tail_tiles,
):
    which = half_ref[0]
    half = rows // 2
    left = left_lanes(half)
    owners = out_ref.shape[0]
    tail_lines = 2 * tail_tiles
    width, tail_width = tiles * LANES, tail_tiles * LANES

    def fetch(start, at, size, number):
        start = pl.multiple_of(start, LANES)
        copy = pltpu.make_async_copy(
            archive_hbm.at[:, pl.ds(start, size)], archive_ref.at[:, pl.ds(at, size)], get_sems.at[number]
        )
        copy.start()
        return copy

    tail_fetch = fetch(2 * width + which * tail_width, width, tail_width, PARTS)
    part_width = width // PARTS
    fetches = [fetch(which * width + part * part_width, part * part_width, part_width, part) for part in range(PARTS)]
    slots = slot_ref[...]
    target, place = slots // rows, slots % rows
    before = lax.broadcasted_iota(jnp.int32, (rows, rows), 0)
    after = lax.broadcasted_iota(jnp.int32, (rows, rows), 1)
    across = jnp.broadcast_to(target, (rows, rows))
    down = jnp.sum(jnp.where(before == after, across, 0), axis=1, keepdims=True)
    rank = jnp.sum(jnp.where((across == down) & (before < after), 1, 0), axis=0, keepdims=True)
    base_vmem[0:1, 0:rows] = target * 2 + rank
    base_copy = pltpu.make_async_copy(base_vmem, base_ref, base_sem)
    base_copy.start()
    info = jnp.concatenate([target, place + rows * rank], axis=1).astype(jnp.float32)
    info = jnp.broadcast_to(info, (8, LANES))
    tail_ref[...] = jnp.zeros_like(tail_ref)
    tail_fetch.wait()
    base_copy.wait()
    for tile in range(tail_tiles):
        at = width + tile * LANES
        block = archive_ref[:, at : at + LANES].astype(jnp.float32)
        for row in range(rows):
            tail_ref[pl.ds(base_ref[0, row] * tail_tiles + tile, 1), :] = block[row : row + 1, :]

    def one(tile, carry):
        at = pl.multiple_of(tile * LANES, LANES)
        block = archive_ref[:, pl.ds(at, LANES)].astype(jnp.float32)
        upper, lower = block[:half], block[half:]
        even = jnp.where(left, upper, roll_half(lower))
        odd = jnp.where(left, roll_half(upper), lower)
        for side, lines in ((0, even), (1, odd)):
            owner = 2 * tile + side
            tail = tail_ref[pl.ds(pl.multiple_of(owner * tail_lines, 8), tail_lines), :]
            out_ref[owner] = jnp.concatenate([lines, tail, info], axis=0).astype(jnp.bfloat16)
        return carry

    copies = []
    for part in range(PARTS):
        fetches[part].wait()
        lax.fori_loop(part * tiles // PARTS, (part + 1) * tiles // PARTS, one, 0, unroll=8)
        copies.append(send_part(out_ref, out_hbm, part, owners // PARTS, sems.at[part]))
    for copy in copies:
        copy.wait()


def permute_kernel(
    owner_ref, got_ref, out_hbm, tail_out_ref,
    out_ref, plain_ref, placed_ref, tail_ref, tail_rows_ref, info_ref, route_ref, route_smem, route_sem, sems,
    *, rows, tail_tiles,
):
    stations = got_ref.shape[0]
    half = rows // 2
    left = left_lanes(half)
    tail_lines = 2 * tail_tiles

    def note(station, carry):
        info_ref[pl.ds(station, 1), :] = got_ref[station][half + tail_lines : half + tail_lines + 8].astype(
            jnp.float32
        )[:1]
        return carry

    lax.fori_loop(0, stations, note, 0, unroll=8)
    info = info_ref[...].astype(jnp.int32)
    other = pltpu.roll(info_ref[...], rows, 1).astype(jnp.int32)
    on_left = lax.broadcasted_iota(jnp.int32, info.shape, 1) < rows
    target = jnp.where(on_left, info, other)
    packed = jnp.where(on_left, other, info)
    place, rank = packed % rows, packed // rows
    mine = target == owner_ref[0]
    first = jnp.max(jnp.where(mine & (rank == 0), place, -1), axis=1, keepdims=True)
    second = jnp.max(jnp.where(mine & (rank == 1), place, -1), axis=1, keepdims=True)
    lane = lax.broadcasted_iota(jnp.int32, info.shape, 1)
    kept = jnp.where(lane == rows, first, second)
    kept = jnp.where(kept < 0, rows, kept)
    route_ref[...] = jnp.where(on_left, target * rows + place, kept)
    route_copy = pltpu.make_async_copy(route_ref, route_smem, route_sem)
    route_copy.start()

    def expand(station, carry):
        block = got_ref[station].astype(jnp.float32)
        lines = block[:half]
        at = pl.multiple_of(station * rows, 8)
        plain_ref[pl.ds(at, half), :] = lines
        plain_ref[pl.ds(at + half, half), :] = roll_half(lines)
        tail_ref[pl.ds(pl.multiple_of(station * tail_lines, 8), tail_lines), :] = block[half : half + tail_lines]
        return carry

    lax.fori_loop(0, stations, expand, 0, unroll=8)
    route_copy.wait()

    def move(station, carry):
        lines = plain_ref[pl.ds(pl.multiple_of(station * rows, 8), rows), :]
        for row in range(rows):
            placed_ref[pl.ds(route_smem[station, row], 1), :] = lines[row : row + 1, :]
        return carry

    lax.fori_loop(0, stations, move, 0)

    def join(station, carry):
        at = pl.multiple_of(station * rows, 8)
        lines = jnp.where(left, placed_ref[pl.ds(at, half), :], roll_half(placed_ref[pl.ds(at + half, half), :]))
        out_ref[station] = lines.astype(jnp.bfloat16)
        return carry

    copies = []
    for part in range(PARTS):
        lax.fori_loop(part * stations // PARTS, (part + 1) * stations // PARTS, join, 0, unroll=8)
        for which in range(2):
            copies.append(
                send_part(out_ref, out_hbm.at[:, which], part, stations // PARTS, sems.at[which, part])
            )
    def keep(station, carry):
        for rank in range(2):
            row = route_smem[station, rows + rank]
            for tile in range(tail_tiles):
                line = station * tail_lines + rank * tail_tiles + tile
                tail_rows_ref[tile, pl.ds(row, 1), :] = tail_ref[pl.ds(line, 1), :]
        return carry

    lax.fori_loop(0, stations, keep, 0, unroll=8)
    for tile in range(tail_tiles):
        tail_out_ref[:, tile * LANES : (tile + 1) * LANES] = tail_rows_ref[tile, :rows, :].astype(jnp.bfloat16)
    for copy in copies:
        copy.wait()


def assemble_kernel(got_ref, tail_low_ref, tail_high_ref, out_hbm, out_ref, sems, *, tiles):
    half = got_ref.shape[1]
    left = left_lanes(half)
    copies = []

    def send(start, size):
        at = (slice(None), pl.ds(start, size))
        copies.append(pltpu.make_async_copy(out_ref.at[at], out_hbm.at[at], sems.at[len(copies)]))
        copies[-1].start()

    at = 2 * tiles * LANES
    width = tail_low_ref.shape[1]
    out_ref[:, at : at + width] = tail_low_ref[...]
    out_ref[:, at + width : at + 2 * width] = tail_high_ref[...]
    send(at, 2 * width)
    for which in range(2):

        def one(tile, carry, which=which):
            even = got_ref[4 * tile + which].astype(jnp.float32)
            odd = got_ref[4 * tile + 2 + which].astype(jnp.float32)
            upper = jnp.where(left, even, roll_half(odd))
            lower = jnp.where(left, roll_half(even), odd)
            at = pl.multiple_of((which * tiles + tile) * LANES, LANES)
            out_ref[:, pl.ds(at, LANES)] = jnp.concatenate([upper, lower], axis=0).astype(jnp.bfloat16)
            return carry

        part = tiles // 2
        for start in range(0, tiles, part):
            lax.fori_loop(start, start + part, one, 0, unroll=8)
            send((which * tiles + start) * LANES, part * LANES)
    for copy in copies:
        copy.wait()


def halving_bits(sizes):
    ys, zs, xs, cores = (size.bit_length() - 1 for size in sizes)
    x_from, z_from, y_from = cores, cores + xs, cores + xs + zs
    return (
        list(range(cores))
        + list(range(y_from, y_from + ys))
        + list(range(x_from, z_from))
        + list(reversed(range(z_from, y_from)))
    )


def place_of(index, bits):
    place = 0
    for at, bit in enumerate(bits):
        place = place + ((index >> bit) & 1) * (1 << (len(bits) - 1 - at))
    return place


def correlate_kernel(
    count_ref, entry_ref, row_ref, shift_ref, place_ref, archive_ref, wave_ref, out_ref,
    series_ref, line_ref, high_ref, low_ref, group_ref, *, length, bits,
):
    rows = archive_ref.shape[0]
    tiles = archive_ref.shape[1] // LANES
    blocks = LANES
    padded = series_ref.shape[0]

    def widen(tile, carry):
        at = pl.multiple_of(tile * LANES, LANES)
        series_ref[tile] = archive_ref[:, pl.ds(at, LANES)].astype(jnp.float32)
        return carry

    lax.fori_loop(0, tiles, widen, 0, unroll=8)
    for tile in range(tiles, padded):
        series_ref[tile] = jnp.zeros((rows, LANES), jnp.float32)
    out_ref[...] = jnp.zeros_like(out_ref)
    line_ref[...] = jnp.zeros_like(line_ref)
    my_place = place_ref[0]
    lag = lax.broadcasted_iota(jnp.int32, (LANES, SPAN), 1) - lax.broadcasted_iota(jnp.int32, (LANES, SPAN), 0)
    contract = (((1,), (1,)), ((), ()))

    def one(step, carry):
        entry = entry_ref[step]
        row = row_ref[entry]
        shift = shift_ref[entry]
        skip, fine = shift // LANES, shift % LANES
        for tile in range(blocks + KW - 1):
            line_ref[tile : tile + 1, :] = series_ref[skip + tile, pl.ds(row, 1), :]
        lines = line_ref[...]
        squares = lines * lines
        high = squares.astype(jnp.bfloat16).astype(jnp.float32)
        high_ref[...] = high
        low_ref[...] = squares - high
        def windows(ref):
            return jnp.concatenate(
                [ref[k : k + blocks, :].astype(jnp.bfloat16) for k in range(KW)], axis=1
            )

        group = pl.multiple_of(entry // GROUP * GROUP, GROUP)
        group_ref[...] = wave_ref[pl.ds(group, GROUP), :].astype(jnp.float32)
        wave = jnp.concatenate(
            [group_ref[pl.ds(entry % GROUP, 1), :], jnp.zeros((1, SPAN - length), jnp.float32)], axis=1
        )
        power = jnp.sum(wave * wave, axis=1, keepdims=True)
        base = pltpu.roll(jnp.broadcast_to(wave, (8, SPAN)), fine, 1)
        banded = pltpu.roll(
            jnp.concatenate([base] * (LANES // 8), axis=0), 0, 1, stride=1, stride_axis=0
        ).astype(jnp.bfloat16)
        inside = (lag >= fine) & (lag < fine + length)
        mask = jnp.where(inside, 1.0, 0.0).astype(jnp.bfloat16)
        product = lax.dot_general(windows(line_ref), banded, contract, preferred_element_type=jnp.float32)
        energy = lax.dot_general(
            windows(high_ref), mask, contract, preferred_element_type=jnp.float32
        ) + lax.dot_general(windows(low_ref), mask, contract, preferred_element_type=jnp.float32)
        scale = (energy / length + EPSILON) * (power / length + EPSILON)
        normalized = product / length / jnp.sqrt(scale)
        template = entry % out_ref.shape[1]
        for block in range(blocks):
            at = (place_of(block, bits) ^ my_place, pl.ds(template, 1), slice(None))
            out_ref[at] = out_ref[at] + normalized[block : block + 1, :]
        return carry

    lax.fori_loop(0, count_ref[0], one, 0)


VMEM_SPEC = pl.BlockSpec(memory_space=pltpu.VMEM)
SMEM_SPEC = pl.BlockSpec(memory_space=pltpu.SMEM)
HBM_SPEC = pl.BlockSpec(memory_space=pltpu.HBM)


def kernel_call(
    body, scalars, arrays, outs, scratch, flops, moved, vmem, out_specs=VMEM_SPEC, in_specs=None
):
    return pl.pallas_call(
        body,
        out_shape=outs,
        in_specs=[SMEM_SPEC] * len(scalars) + (in_specs or [VMEM_SPEC] * len(arrays)),
        out_specs=out_specs,
        scratch_shapes=scratch,
        compiler_params=pltpu.CompilerParams(vmem_limit_bytes=vmem * MIB),
        cost_estimate=pl.CostEstimate(flops=flops, bytes_accessed=moved, transcendentals=0),
    )(*scalars, *arrays)


def halve(partial, bit, count):
    half = partial.shape[0] // 2
    pairs = [(i, i ^ (1 << bit)) for i in range(count)]
    return partial[:half] + lax.ppermute(partial[half:], "stn", pairs)


def exchange(partial, bits, count):
    total = partial[0]
    for block in range(1, partial.shape[0]):
        mask = sum(1 << bit for at, bit in enumerate(bits) if block >> (len(bits) - 1 - at) & 1)
        total = total + lax.ppermute(partial[block], "stn", [(i, i ^ mask) for i in range(count)])
    return total


def owned_entries(slots, template_channels):
    flat = template_channels.reshape(-1)
    count = flat.shape[0]
    match = (flat[None, :] == slots[:, None]).astype(jnp.int32)
    row = jnp.sum(match * jnp.arange(slots.shape[0], dtype=jnp.int32)[:, None], axis=0)
    here = jnp.sum(match, axis=0)
    number = jnp.arange(count, dtype=jnp.int32)
    before = jnp.sum(jnp.where(number[None, :] < number[:, None], here[None, :], 0), axis=1)
    where_to = jnp.where(here > 0, before, count)
    entries = jnp.sum(jnp.where(where_to[None, :] == number[:, None], number[None, :], 0), axis=1)
    return entries, row, jnp.sum(here).reshape(1)


def shards(archive, slot_of_row, templates, template_channels, moveouts, *, sizes):
    stations = lax.axis_size("stn")
    my_index = lax.axis_index("stn")
    which = lax.axis_index("tpl").astype(jnp.int32)
    rows, samples = archive.shape
    half = rows // 2
    local_templates, channels, length = templates.shape
    tiles = stations // 2
    tail_tiles = (samples // LANES - 2 * tiles) // 2
    block_lines = half + 2 * tail_tiles + 8
    f32, bf16, i32 = jnp.float32, jnp.bfloat16, jnp.int32
    shape = jax.ShapeDtypeStruct

    packed = kernel_call(
        functools.partial(pack_kernel, rows=rows, tiles=tiles, tail_tiles=tail_tiles),
        (which.reshape(1),),
        (slot_of_row.reshape(1, rows), archive),
        shape((stations, block_lines, LANES), bf16),
        [
            pltpu.VMEM((rows, (tiles + tail_tiles) * LANES), bf16),
            pltpu.VMEM((stations, block_lines, LANES), bf16),
            pltpu.VMEM((stations * 2 * tail_tiles, LANES), f32),
            pltpu.VMEM((8, LANES), i32),
            pltpu.SMEM((8, LANES), i32),
            pltpu.SemaphoreType.DMA((PARTS + 1,)),
            pltpu.SemaphoreType.DMA((PARTS,)),
            pltpu.SemaphoreType.DMA,
        ],
        4_000_000, 4_000_000, 56, HBM_SPEC, [VMEM_SPEC, HBM_SPEC],
    )
    packed, later_archive = lax.optimization_barrier((packed, archive))
    first = lax.all_to_all(packed, "stn", 0, 0, tiled=True)

    entries, entry_row, entry_count = owned_entries(slot_of_row, template_channels.T)
    waves = templates.transpose(1, 0, 2).reshape(-1, length)
    padded = samples // LANES + 8
    bits = halving_bits(sizes)
    my_place = place_of(my_index.astype(i32), bits).reshape(1)
    partial = kernel_call(
        functools.partial(correlate_kernel, length=length, bits=bits),
        (entry_count, entries, entry_row, moveouts.T.reshape(-1), my_place),
        (later_archive, waves),
        shape((stations, local_templates, LANES), f32),
        [
            pltpu.VMEM((padded, rows, LANES), f32),
            pltpu.VMEM((LANES + 8, LANES), f32),
            pltpu.VMEM((LANES + 8, LANES), f32),
            pltpu.VMEM((LANES + 8, LANES), f32),
            pltpu.VMEM((GROUP, length), f32),
        ],
        1000, 1000, 28,
    )
    partial = halve(partial, bits[0], stations)
    first, partial = lax.optimization_barrier((first, partial))
    partial = halve(partial, bits[1], stations)

    lines, tail_rows = kernel_call(
        functools.partial(permute_kernel, rows=rows, tail_tiles=tail_tiles),
        (my_index.astype(i32).reshape(1),),
        (first,),
        (shape((stations, 2, half, LANES), bf16), shape((rows, tail_tiles * LANES), bf16)),
        [
            pltpu.VMEM((stations, half, LANES), bf16),
            pltpu.VMEM((stations * rows, LANES), f32),
            pltpu.VMEM((stations * rows, LANES), f32),
            pltpu.VMEM((stations * 2 * tail_tiles, LANES), f32),
            pltpu.VMEM((tail_tiles, rows + 8, LANES), f32),
            pltpu.VMEM((stations, LANES), f32),
            pltpu.VMEM((stations, LANES), i32),
            pltpu.SMEM((stations, LANES), i32),
            pltpu.SemaphoreType.DMA,
            pltpu.SemaphoreType.DMA((2, PARTS)),
        ],
        4_000_000, 30_000_000, 52, (HBM_SPEC, VMEM_SPEC),
    )
    lines, _ = lax.optimization_barrier((lines, partial))
    lines = lines.reshape(2 * stations, half, LANES)
    second = lax.all_to_all(lines, ("stn", "tpl"), 0, 0, tiled=True)
    for bit in bits[2:-3]:
        partial = halve(partial, bit, stations)
    stack = exchange(partial, bits[-3:], stations) * math.sqrt(length / channels)
    tail_other = lax.ppermute(tail_rows, "tpl", [(0, 1), (1, 0)])
    tail_low = jnp.where(which == 0, tail_rows, tail_other)
    tail_high = jnp.where(which == 0, tail_other, tail_rows)
    grouped = kernel_call(
        functools.partial(assemble_kernel, tiles=tiles),
        (),
        (second, tail_low, tail_high),
        shape((rows, samples), bf16),
        [pltpu.VMEM((rows, samples), bf16), pltpu.SemaphoreType.DMA((5,))],
        4_000_000, 6_000_000, 12, HBM_SPEC,
    )
    return grouped, stack


def solution(mesh):
    sizes = (2, 8, 4, 2)
    in_specs = (P("stn", None), P("stn"), P("tpl", None, None), P("tpl", None), P("tpl", None))
    out_specs = (P("stn", None), P("tpl", "stn"))
    return jax.shard_map(
        functools.partial(shards, sizes=sizes), mesh=mesh, in_specs=in_specs, out_specs=out_specs, check_vma=False
    )
```

```python
import functools
import math

import jax
import jax.numpy as jnp
from jax import lax
from jax.experimental import pallas as pl
from jax.experimental.pallas import tpu as pltpu
from jax.sharding import PartitionSpec as P

EPSILON = 1e-06
LANES = 128
KW = 7
SPAN = KW * LANES
MIB = 1024 * 1024
PARTS = 4
GROUP = 16
EARLY = 2


def roll_half(x):
    return pltpu.roll(x, LANES // 2, 1)


def left_lanes(rows):
    return lax.broadcasted_iota(jnp.int32, (rows, LANES), 1) < LANES // 2


def send_part(source, target, part, size, sem):
    at = pl.ds(part * size, size)
    copy = pltpu.make_async_copy(source.at[at], target.at[at], sem)
    copy.start()
    return copy


def pack_kernel(
    half_ref, slot_ref, archive_hbm, out_hbm, archive_ref, out_ref, tail_ref, base_vmem, base_ref, get_sems, sems, base_sem,
    *, rows, tiles, tail_tiles,
):
    which = half_ref[0]
    half = rows // 2
    left = left_lanes(half)
    owners = out_ref.shape[0]
    tail_lines = 2 * tail_tiles
    width, tail_width = tiles * LANES, tail_tiles * LANES

    def fetch(start, at, size, number):
        start = pl.multiple_of(start, LANES)
        copy = pltpu.make_async_copy(
            archive_hbm.at[:, pl.ds(start, size)], archive_ref.at[:, pl.ds(at, size)], get_sems.at[number]
        )
        copy.start()
        return copy

    tail_fetch = fetch(2 * width + which * tail_width, width, tail_width, PARTS)
    part_width = width // PARTS
    fetches = [fetch(which * width + part * part_width, part * part_width, part_width, part) for part in range(PARTS)]
    slots = slot_ref[...]
    target, place = slots // rows, slots % rows
    before = lax.broadcasted_iota(jnp.int32, (rows, rows), 0)
    after = lax.broadcasted_iota(jnp.int32, (rows, rows), 1)
    across = jnp.broadcast_to(target, (rows, rows))
    down = jnp.sum(jnp.where(before == after, across, 0), axis=1, keepdims=True)
    rank = jnp.sum(jnp.where((across == down) & (before < after), 1, 0), axis=0, keepdims=True)
    base_vmem[0:1, 0:rows] = target * 2 + rank
    base_copy = pltpu.make_async_copy(base_vmem, base_ref, base_sem)
    base_copy.start()
    info = jnp.concatenate([target, place + rows * rank], axis=1).astype(jnp.float32)
    info = jnp.broadcast_to(info, (8, LANES))
    tail_ref[...] = jnp.zeros_like(tail_ref)
    tail_fetch.wait()
    base_copy.wait()
    for tile in range(tail_tiles):
        at = width + tile * LANES
        block = archive_ref[:, at : at + LANES].astype(jnp.float32)
        for row in range(rows):
            tail_ref[pl.ds(base_ref[0, row] * tail_tiles + tile, 1), :] = block[row : row + 1, :]

    def one(tile, carry):
        at = pl.multiple_of(tile * LANES, LANES)
        block = archive_ref[:, pl.ds(at, LANES)].astype(jnp.float32)
        upper, lower = block[:half], block[half:]
        even = jnp.where(left, upper, roll_half(lower))
        odd = jnp.where(left, roll_half(upper), lower)
        for side, lines in ((0, even), (1, odd)):
            owner = 2 * tile + side
            tail = tail_ref[pl.ds(pl.multiple_of(owner * tail_lines, 8), tail_lines), :]
            out_ref[owner] = jnp.concatenate([lines, tail, info], axis=0).astype(jnp.bfloat16)
        return carry

    copies = []
    for part in range(PARTS):
        fetches[part].wait()
        lax.fori_loop(part * tiles // PARTS, (part + 1) * tiles // PARTS, one, 0, unroll=8)
        copies.append(send_part(out_ref, out_hbm, part, owners // PARTS, sems.at[part]))
    for copy in copies:
        copy.wait()


def permute_kernel(
    owner_ref, got_ref, out_hbm, tail_out_ref,
    out_ref, plain_ref, placed_ref, tail_ref, tail_rows_ref, info_ref, route_ref, route_smem, route_sems, sems,
    *, rows, tail_tiles,
):
    stations = got_ref.shape[0]
    half = rows // 2
    left = left_lanes(half)
    tail_lines = 2 * tail_tiles

    def note(station, carry):
        info_ref[pl.ds(station, 1), :] = got_ref[station][half + tail_lines : half + tail_lines + 8].astype(
            jnp.float32
        )[:1]
        return carry

    lax.fori_loop(0, stations, note, 0, unroll=8)
    info = info_ref[...].astype(jnp.int32)
    other = pltpu.roll(info_ref[...], rows, 1).astype(jnp.int32)
    on_left = lax.broadcasted_iota(jnp.int32, info.shape, 1) < rows
    target = jnp.where(on_left, info, other)
    packed = jnp.where(on_left, other, info)
    place, rank = packed % rows, packed // rows
    mine = target == owner_ref[0]
    first = jnp.max(jnp.where(mine & (rank == 0), place, -1), axis=1, keepdims=True)
    second = jnp.max(jnp.where(mine & (rank == 1), place, -1), axis=1, keepdims=True)
    lane = lax.broadcasted_iota(jnp.int32, info.shape, 1)
    kept = jnp.where(lane == rows, first, second)
    kept = jnp.where(kept < 0, rows, kept)
    route_ref[...] = jnp.where(on_left, target * rows + place, kept)
    share = stations // PARTS
    route_copies = [send_part(route_ref, route_smem, part, share, route_sems.at[part]) for part in range(PARTS)]

    def expand(station, carry):
        block = got_ref[station].astype(jnp.float32)
        lines = block[:half]
        at = pl.multiple_of(station * rows, 8)
        plain_ref[pl.ds(at, half), :] = lines
        plain_ref[pl.ds(at + half, half), :] = roll_half(lines)
        tail_ref[pl.ds(pl.multiple_of(station * tail_lines, 8), tail_lines), :] = block[half : half + tail_lines]
        return carry

    lax.fori_loop(0, stations, expand, 0, unroll=8)

    def move(station, carry):
        lines = plain_ref[pl.ds(pl.multiple_of(station * rows, 8), rows), :]
        for row in range(rows):
            placed_ref[pl.ds(route_smem[station, row], 1), :] = lines[row : row + 1, :]
        return carry

    for part in range(PARTS):
        route_copies[part].wait()
        lax.fori_loop(part * share, (part + 1) * share, move, 0, unroll=4)

    def join(station, carry):
        at = pl.multiple_of(station * rows, 8)
        lines = jnp.where(left, placed_ref[pl.ds(at, half), :], roll_half(placed_ref[pl.ds(at + half, half), :]))
        out_ref[station] = lines.astype(jnp.bfloat16)
        return carry

    copies = []
    for part in range(PARTS):
        lax.fori_loop(part * stations // PARTS, (part + 1) * stations // PARTS, join, 0, unroll=16)
        for which in range(2):
            copies.append(
                send_part(out_ref, out_hbm.at[:, which], part, stations // PARTS, sems.at[which, part])
            )
    def keep(station, carry):
        for rank in range(2):
            row = route_smem[station, rows + rank]
            for tile in range(tail_tiles):
                line = station * tail_lines + rank * tail_tiles + tile
                tail_rows_ref[tile, pl.ds(row, 1), :] = tail_ref[pl.ds(line, 1), :]
        return carry

    lax.fori_loop(0, stations, keep, 0, unroll=8)
    for tile in range(tail_tiles):
        tail_out_ref[:, tile * LANES : (tile + 1) * LANES] = tail_rows_ref[tile, :rows, :].astype(jnp.bfloat16)
    for copy in copies:
        copy.wait()


def assemble_kernel(got_ref, tail_low_ref, tail_high_ref, out_hbm, out_ref, sems, *, tiles):
    half = got_ref.shape[1]
    left = left_lanes(half)
    copies = []

    def send(start, size):
        at = (slice(None), pl.ds(start, size))
        copies.append(pltpu.make_async_copy(out_ref.at[at], out_hbm.at[at], sems.at[len(copies)]))
        copies[-1].start()

    at = 2 * tiles * LANES
    width = tail_low_ref.shape[1]
    out_ref[:, at : at + width] = tail_low_ref[...]
    out_ref[:, at + width : at + 2 * width] = tail_high_ref[...]
    send(at, 2 * width)
    for which in range(2):

        def one(tile, carry, which=which):
            even = got_ref[4 * tile + which].astype(jnp.float32)
            odd = got_ref[4 * tile + 2 + which].astype(jnp.float32)
            upper = jnp.where(left, even, roll_half(odd))
            lower = jnp.where(left, roll_half(even), odd)
            at = pl.multiple_of((which * tiles + tile) * LANES, LANES)
            out_ref[:, pl.ds(at, LANES)] = jnp.concatenate([upper, lower], axis=0).astype(jnp.bfloat16)
            return carry

        part = tiles // 2
        for start in range(0, tiles, part):
            lax.fori_loop(start, start + part, one, 0, unroll=8)
            send((which * tiles + start) * LANES, part * LANES)
    for copy in copies:
        copy.wait()


def halving_bits(sizes):
    ys, zs, xs, cores = (size.bit_length() - 1 for size in sizes)
    x_from, z_from, y_from = cores, cores + xs, cores + xs + zs
    return (
        list(range(cores))
        + list(range(y_from, y_from + ys))
        + list(range(x_from, z_from))
        + list(reversed(range(z_from, y_from)))
    )


def place_of(index, bits):
    place = 0
    for at, bit in enumerate(bits):
        place = place + ((index >> bit) & 1) * (1 << (len(bits) - 1 - at))
    return place


def correlate_kernel(
    count_ref, entry_ref, row_ref, shift_ref, place_ref, archive_ref, wave_ref, out_ref,
    series_ref, line_ref, high_ref, low_ref, group_ref, *, length, bits,
):
    rows = archive_ref.shape[0]
    tiles = archive_ref.shape[1] // LANES
    blocks = LANES
    padded = series_ref.shape[0]

    def widen(tile, carry):
        at = pl.multiple_of(tile * LANES, LANES)
        series_ref[tile] = archive_ref[:, pl.ds(at, LANES)].astype(jnp.float32)
        return carry

    lax.fori_loop(0, tiles, widen, 0, unroll=8)
    for tile in range(tiles, padded):
        series_ref[tile] = jnp.zeros((rows, LANES), jnp.float32)
    out_ref[...] = jnp.zeros_like(out_ref)
    line_ref[...] = jnp.zeros_like(line_ref)
    my_place = place_ref[0]
    lag = lax.broadcasted_iota(jnp.int32, (LANES, SPAN), 1) - lax.broadcasted_iota(jnp.int32, (LANES, SPAN), 0)
    contract = (((1,), (1,)), ((), ()))

    def one(step, carry):
        entry = entry_ref[step]
        row = row_ref[entry]
        shift = shift_ref[entry]
        skip, fine = shift // LANES, shift % LANES
        for tile in range(blocks + KW - 1):
            line_ref[tile : tile + 1, :] = series_ref[skip + tile, pl.ds(row, 1), :]
        lines = line_ref[...]
        squares = lines * lines
        high = squares.astype(jnp.bfloat16).astype(jnp.float32)
        high_ref[...] = high
        low_ref[...] = squares - high
        def windows(ref):
            return jnp.concatenate(
                [ref[k : k + blocks, :].astype(jnp.bfloat16) for k in range(KW)], axis=1
            )

        group = pl.multiple_of(entry // GROUP * GROUP, GROUP)
        group_ref[...] = wave_ref[pl.ds(group, GROUP), :].astype(jnp.float32)
        wave = jnp.concatenate(
            [group_ref[pl.ds(entry % GROUP, 1), :], jnp.zeros((1, SPAN - length), jnp.float32)], axis=1
        )
        power = jnp.sum(wave * wave, axis=1, keepdims=True)
        base = pltpu.roll(jnp.broadcast_to(wave, (8, SPAN)), fine, 1)
        banded = pltpu.roll(
            jnp.concatenate([base] * (LANES // 8), axis=0), 0, 1, stride=1, stride_axis=0
        ).astype(jnp.bfloat16)
        inside = (lag >= fine) & (lag < fine + length)
        mask = jnp.where(inside, 1.0, 0.0).astype(jnp.bfloat16)
        product = lax.dot_general(windows(line_ref), banded, contract, preferred_element_type=jnp.float32)
        energy = lax.dot_general(
            windows(high_ref), mask, contract, preferred_element_type=jnp.float32
        ) + lax.dot_general(windows(low_ref), mask, contract, preferred_element_type=jnp.float32)
        scale = (energy / length + EPSILON) * (power / length + EPSILON)
        normalized = product / length / jnp.sqrt(scale)
        template = entry % out_ref.shape[1]
        for block in range(blocks):
            at = (place_of(block, bits) ^ my_place, pl.ds(template, 1), slice(None))
            out_ref[at] = out_ref[at] + normalized[block : block + 1, :]
        return carry

    lax.fori_loop(0, count_ref[0], one, 0)


VMEM_SPEC = pl.BlockSpec(memory_space=pltpu.VMEM)
SMEM_SPEC = pl.BlockSpec(memory_space=pltpu.SMEM)
HBM_SPEC = pl.BlockSpec(memory_space=pltpu.HBM)


def kernel_call(
    body, scalars, arrays, outs, scratch, flops, moved, vmem, out_specs=VMEM_SPEC, in_specs=None
):
    return pl.pallas_call(
        body,
        out_shape=outs,
        in_specs=[SMEM_SPEC] * len(scalars) + (in_specs or [VMEM_SPEC] * len(arrays)),
        out_specs=out_specs,
        scratch_shapes=scratch,
        compiler_params=pltpu.CompilerParams(vmem_limit_bytes=vmem * MIB),
        cost_estimate=pl.CostEstimate(flops=flops, bytes_accessed=moved, transcendentals=0),
    )(*scalars, *arrays)


def halve(partial, bit, count):
    half = partial.shape[0] // 2
    pairs = [(i, i ^ (1 << bit)) for i in range(count)]
    return partial[:half] + lax.ppermute(partial[half:], "stn", pairs)


def exchange(partial, bits, count):
    parts = 1 << len(bits)
    partial = partial.reshape((parts, partial.shape[0] // parts) + partial.shape[1:])
    total = partial[0]
    for part in range(1, parts):
        mask = sum(1 << bit for at, bit in enumerate(bits) if part >> (len(bits) - 1 - at) & 1)
        total = total + lax.ppermute(partial[part], "stn", [(i, i ^ mask) for i in range(count)])
    return total


def owned_entries(slots, template_channels):
    flat = template_channels.reshape(-1)
    count = flat.shape[0]
    match = (flat[None, :] == slots[:, None]).astype(jnp.int32)
    row = jnp.sum(match * jnp.arange(slots.shape[0], dtype=jnp.int32)[:, None], axis=0)
    here = jnp.sum(match, axis=0)
    number = jnp.arange(count, dtype=jnp.int32)
    before = jnp.sum(jnp.where(number[None, :] < number[:, None], here[None, :], 0), axis=1)
    where_to = jnp.where(here > 0, before, count)
    entries = jnp.sum(jnp.where(where_to[None, :] == number[:, None], number[None, :], 0), axis=1)
    return entries, row, jnp.sum(here).reshape(1)


def shards(archive, slot_of_row, templates, template_channels, moveouts, *, sizes):
    stations = lax.axis_size("stn")
    my_index = lax.axis_index("stn")
    which = lax.axis_index("tpl").astype(jnp.int32)
    rows, samples = archive.shape
    half = rows // 2
    local_templates, channels, length = templates.shape
    tiles = stations // 2
    tail_tiles = (samples // LANES - 2 * tiles) // 2
    block_lines = half + 2 * tail_tiles + 8
    f32, bf16, i32 = jnp.float32, jnp.bfloat16, jnp.int32
    shape = jax.ShapeDtypeStruct

    packed = kernel_call(
        functools.partial(pack_kernel, rows=rows, tiles=tiles, tail_tiles=tail_tiles),
        (which.reshape(1),),
        (slot_of_row.reshape(1, rows), archive),
        shape((stations, block_lines, LANES), bf16),
        [
            pltpu.VMEM((rows, (tiles + tail_tiles) * LANES), bf16),
            pltpu.VMEM((stations, block_lines, LANES), bf16),
            pltpu.VMEM((stations * 2 * tail_tiles, LANES), f32),
            pltpu.VMEM((8, LANES), i32),
            pltpu.SMEM((8, LANES), i32),
            pltpu.SemaphoreType.DMA((PARTS + 1,)),
            pltpu.SemaphoreType.DMA((PARTS,)),
            pltpu.SemaphoreType.DMA,
        ],
        4_000_000, 4_000_000, 56, HBM_SPEC, [VMEM_SPEC, HBM_SPEC],
    )
    packed, later_archive = lax.optimization_barrier((packed, archive))
    first = lax.all_to_all(packed, "stn", 0, 0, tiled=True)

    entries, entry_row, entry_count = owned_entries(slot_of_row, template_channels.T)
    waves = templates.transpose(1, 0, 2).reshape(-1, length)
    padded = samples // LANES + 8
    bits = halving_bits(sizes)
    my_place = place_of(my_index.astype(i32), bits).reshape(1)
    partial = kernel_call(
        functools.partial(correlate_kernel, length=length, bits=bits),
        (entry_count, entries, entry_row, moveouts.T.reshape(-1), my_place),
        (later_archive, waves),
        shape((stations, local_templates, LANES), f32),
        [
            pltpu.VMEM((padded, rows, LANES), f32),
            pltpu.VMEM((LANES + 8, LANES), f32),
            pltpu.VMEM((LANES + 8, LANES), f32),
            pltpu.VMEM((LANES + 8, LANES), f32),
            pltpu.VMEM((GROUP, length), f32),
        ],
        1000, 1000, 28,
    )
    for bit in bits[:EARLY]:
        partial = halve(partial, bit, stations)
    first, _ = lax.optimization_barrier((first, partial))

    lines, tail_rows = kernel_call(
        functools.partial(permute_kernel, rows=rows, tail_tiles=tail_tiles),
        (my_index.astype(i32).reshape(1),),
        (first,),
        (shape((stations, 2, half, LANES), bf16), shape((rows, tail_tiles * LANES), bf16)),
        [
            pltpu.VMEM((stations, half, LANES), bf16),
            pltpu.VMEM((stations * rows, LANES), f32),
            pltpu.VMEM((stations * rows, LANES), f32),
            pltpu.VMEM((stations * 2 * tail_tiles, LANES), f32),
            pltpu.VMEM((tail_tiles, rows + 8, LANES), f32),
            pltpu.VMEM((stations, LANES), f32),
            pltpu.VMEM((stations, LANES), i32),
            pltpu.SMEM((stations, LANES), i32),
            pltpu.SemaphoreType.DMA((PARTS,)),
            pltpu.SemaphoreType.DMA((2, PARTS)),
        ],
        4_000_000, 30_000_000, 52, (HBM_SPEC, VMEM_SPEC),
    )
    lines = lines.reshape(2 * stations, half, LANES)
    second = lax.all_to_all(lines, ("stn", "tpl"), 0, 0, tiled=True)
    for part in bits[EARLY:-3], bits[-3:]:
        partial = exchange(partial, part, stations)
    stack = partial[0] * math.sqrt(length / channels)
    tail_other = lax.ppermute(tail_rows, "tpl", [(0, 1), (1, 0)])
    tail_low = jnp.where(which == 0, tail_rows, tail_other)
    tail_high = jnp.where(which == 0, tail_other, tail_rows)
    grouped = kernel_call(
        functools.partial(assemble_kernel, tiles=tiles),
        (),
        (second, tail_low, tail_high),
        shape((rows, samples), bf16),
        [pltpu.VMEM((rows, samples), bf16), pltpu.SemaphoreType.DMA((5,))],
        4_000_000, 6_000_000, 12, HBM_SPEC,
    )
    return grouped, stack


def solution(mesh):
    sizes = (2, 8, 4, 2)
    in_specs = (P("stn", None), P("stn"), P("tpl", None, None), P("tpl", None), P("tpl", None))
    out_specs = (P("stn", None), P("tpl", "stn"))
    return jax.shard_map(
        functools.partial(shards, sizes=sizes), mesh=mesh, in_specs=in_specs, out_specs=out_specs, check_vma=False
    )
```

```python
import functools
import math

import jax
import jax.numpy as jnp
from jax import lax
from jax.experimental import pallas as pl
from jax.experimental.pallas import tpu as pltpu
from jax.sharding import PartitionSpec as P

EPSILON = 1e-06
LANES = 128
KW = 7
SPAN = KW * LANES
MIB = 1024 * 1024
PARTS = 4
GROUP = 16
EARLY = 2


def roll_half(x):
    return pltpu.roll(x, LANES // 2, 1)


def left_lanes(rows):
    return lax.broadcasted_iota(jnp.int32, (rows, LANES), 1) < LANES // 2


def send_part(source, target, part, size, sem):
    at = pl.ds(part * size, size)
    copy = pltpu.make_async_copy(source.at[at], target.at[at], sem)
    copy.start()
    return copy


def pack_kernel(
    half_ref, slot_ref, archive_hbm, out_hbm, archive_ref, out_ref, tail_ref, base_vmem, base_ref, get_sems, sems, base_sem,
    *, rows, tiles, tail_tiles,
):
    which = half_ref[0]
    half = rows // 2
    left = left_lanes(half)
    owners = out_ref.shape[0]
    tail_lines = 2 * tail_tiles
    width, tail_width = tiles * LANES, tail_tiles * LANES

    def fetch(start, at, size, number):
        start = pl.multiple_of(start, LANES)
        copy = pltpu.make_async_copy(
            archive_hbm.at[:, pl.ds(start, size)], archive_ref.at[:, pl.ds(at, size)], get_sems.at[number]
        )
        copy.start()
        return copy

    tail_fetch = fetch(2 * width + which * tail_width, width, tail_width, PARTS)
    part_width = width // PARTS
    fetches = [fetch(which * width + part * part_width, part * part_width, part_width, part) for part in range(PARTS)]
    slots = slot_ref[...]
    target, place = slots // rows, slots % rows
    before = lax.broadcasted_iota(jnp.int32, (rows, rows), 0)
    after = lax.broadcasted_iota(jnp.int32, (rows, rows), 1)
    across = jnp.broadcast_to(target, (rows, rows))
    down = jnp.sum(jnp.where(before == after, across, 0), axis=1, keepdims=True)
    rank = jnp.sum(jnp.where((across == down) & (before < after), 1, 0), axis=0, keepdims=True)
    base_vmem[0:1, 0:rows] = target * 2 + rank
    base_copy = pltpu.make_async_copy(base_vmem, base_ref, base_sem)
    base_copy.start()
    info = jnp.concatenate([target, place + rows * rank], axis=1).astype(jnp.float32)
    info = jnp.broadcast_to(info, (8, LANES))
    tail_ref[...] = jnp.zeros_like(tail_ref)
    tail_fetch.wait()
    base_copy.wait()
    for tile in range(tail_tiles):
        at = width + tile * LANES
        block = archive_ref[:, at : at + LANES].astype(jnp.float32)
        for row in range(rows):
            tail_ref[pl.ds(base_ref[0, row] * tail_tiles + tile, 1), :] = block[row : row + 1, :]

    def one(tile, carry):
        at = pl.multiple_of(tile * LANES, LANES)
        block = archive_ref[:, pl.ds(at, LANES)].astype(jnp.float32)
        upper, lower = block[:half], block[half:]
        even = jnp.where(left, upper, roll_half(lower))
        odd = jnp.where(left, roll_half(upper), lower)
        for side, lines in ((0, even), (1, odd)):
            owner = 2 * tile + side
            tail = tail_ref[pl.ds(pl.multiple_of(owner * tail_lines, 8), tail_lines), :]
            out_ref[owner] = jnp.concatenate([lines, tail, info], axis=0).astype(jnp.bfloat16)
        return carry

    copies = []
    for part in range(PARTS):
        fetches[part].wait()
        lax.fori_loop(part * tiles // PARTS, (part + 1) * tiles // PARTS, one, 0, unroll=8)
        copies.append(send_part(out_ref, out_hbm, part, owners // PARTS, sems.at[part]))
    for copy in copies:
        copy.wait()


def permute_kernel(
    owner_ref, got_ref, out_hbm, tail_out_ref,
    out_ref, plain_ref, placed_ref, tail_ref, tail_rows_ref, info_ref, route_ref, route_smem, route_sems, sems,
    *, rows, tail_tiles,
):
    stations = got_ref.shape[0]
    half = rows // 2
    left = left_lanes(half)
    tail_lines = 2 * tail_tiles

    def note(station, carry):
        info_ref[pl.ds(station, 1), :] = got_ref[station][half + tail_lines : half + tail_lines + 8].astype(
            jnp.float32
        )[:1]
        return carry

    lax.fori_loop(0, stations, note, 0, unroll=8)
    info = info_ref[...].astype(jnp.int32)
    other = pltpu.roll(info_ref[...], rows, 1).astype(jnp.int32)
    on_left = lax.broadcasted_iota(jnp.int32, info.shape, 1) < rows
    target = jnp.where(on_left, info, other)
    packed = jnp.where(on_left, other, info)
    place, rank = packed % rows, packed // rows
    mine = target == owner_ref[0]
    first = jnp.max(jnp.where(mine & (rank == 0), place, -1), axis=1, keepdims=True)
    second = jnp.max(jnp.where(mine & (rank == 1), place, -1), axis=1, keepdims=True)
    lane = lax.broadcasted_iota(jnp.int32, info.shape, 1)
    kept = jnp.where(lane == rows, first, second)
    kept = jnp.where(kept < 0, rows, kept)
    route_ref[...] = jnp.where(on_left, target * rows + place, kept)
    share = stations // PARTS
    route_copies = [send_part(route_ref, route_smem, part, share, route_sems.at[part]) for part in range(PARTS)]

    def expand(station, carry):
        block = got_ref[station].astype(jnp.float32)
        lines = block[:half]
        at = pl.multiple_of(station * rows, 8)
        plain_ref[pl.ds(at, half), :] = lines
        plain_ref[pl.ds(at + half, half), :] = roll_half(lines)
        tail_ref[pl.ds(pl.multiple_of(station * tail_lines, 8), tail_lines), :] = block[half : half + tail_lines]
        return carry

    lax.fori_loop(0, stations, expand, 0, unroll=8)

    def move(station, carry):
        lines = plain_ref[pl.ds(pl.multiple_of(station * rows, 8), rows), :]
        for row in range(rows):
            placed_ref[pl.ds(route_smem[station, row], 1), :] = lines[row : row + 1, :]
        return carry

    for part in range(PARTS):
        route_copies[part].wait()
        lax.fori_loop(part * share, (part + 1) * share, move, 0, unroll=4)

    def join(station, carry):
        at = pl.multiple_of(station * rows, 8)
        lines = jnp.where(left, placed_ref[pl.ds(at, half), :], roll_half(placed_ref[pl.ds(at + half, half), :]))
        out_ref[station] = lines.astype(jnp.bfloat16)
        return carry

    copies = []
    for part in range(PARTS):
        lax.fori_loop(part * stations // PARTS, (part + 1) * stations // PARTS, join, 0, unroll=16)
        for which in range(2):
            copies.append(
                send_part(out_ref, out_hbm.at[:, which], part, stations // PARTS, sems.at[which, part])
            )
    def keep(station, carry):
        for rank in range(2):
            row = route_smem[station, rows + rank]
            for tile in range(tail_tiles):
                line = station * tail_lines + rank * tail_tiles + tile
                tail_rows_ref[tile, pl.ds(row, 1), :] = tail_ref[pl.ds(line, 1), :]
        return carry

    lax.fori_loop(0, stations, keep, 0, unroll=8)
    for tile in range(tail_tiles):
        tail_out_ref[:, tile * LANES : (tile + 1) * LANES] = tail_rows_ref[tile, :rows, :].astype(jnp.bfloat16)
    for copy in copies:
        copy.wait()


def assemble_kernel(got_ref, tail_low_ref, tail_high_ref, out_hbm, out_ref, sems, *, tiles):
    half = got_ref.shape[1]
    left = left_lanes(half)
    copies = []

    def send(start, size):
        at = (slice(None), pl.ds(start, size))
        copies.append(pltpu.make_async_copy(out_ref.at[at], out_hbm.at[at], sems.at[len(copies)]))
        copies[-1].start()

    at = 2 * tiles * LANES
    width = tail_low_ref.shape[1]
    out_ref[:, at : at + width] = tail_low_ref[...]
    out_ref[:, at + width : at + 2 * width] = tail_high_ref[...]
    send(at, 2 * width)
    for which in range(2):

        def one(tile, carry, which=which):
            even = got_ref[4 * tile + which].astype(jnp.float32)
            odd = got_ref[4 * tile + 2 + which].astype(jnp.float32)
            upper = jnp.where(left, even, roll_half(odd))
            lower = jnp.where(left, roll_half(even), odd)
            at = pl.multiple_of((which * tiles + tile) * LANES, LANES)
            out_ref[:, pl.ds(at, LANES)] = jnp.concatenate([upper, lower], axis=0).astype(jnp.bfloat16)
            return carry

        part = tiles // 2
        for start in range(0, tiles, part):
            lax.fori_loop(start, start + part, one, 0, unroll=8)
            send((which * tiles + start) * LANES, part * LANES)
    for copy in copies:
        copy.wait()


def halving_bits(sizes):
    ys, zs, xs, cores = (size.bit_length() - 1 for size in sizes)
    x_from, z_from, y_from = cores, cores + xs, cores + xs + zs
    return (
        list(range(cores))
        + list(range(y_from, y_from + ys))
        + [z_from]
        + list(range(x_from, z_from))
        + list(reversed(range(z_from + 1, y_from)))
    )


def place_of(index, bits):
    place = 0
    for at, bit in enumerate(bits):
        place = place + ((index >> bit) & 1) * (1 << (len(bits) - 1 - at))
    return place


def correlate_kernel(
    count_ref, entry_ref, row_ref, shift_ref, place_ref, archive_ref, wave_ref, out_ref,
    series_ref, line_ref, high_ref, low_ref, group_ref, *, length, bits,
):
    rows = archive_ref.shape[0]
    tiles = archive_ref.shape[1] // LANES
    blocks = LANES
    padded = series_ref.shape[0]

    def widen(tile, carry):
        at = pl.multiple_of(tile * LANES, LANES)
        series_ref[tile] = archive_ref[:, pl.ds(at, LANES)].astype(jnp.float32)
        return carry

    lax.fori_loop(0, tiles, widen, 0, unroll=8)
    for tile in range(tiles, padded):
        series_ref[tile] = jnp.zeros((rows, LANES), jnp.float32)
    out_ref[...] = jnp.zeros_like(out_ref)
    line_ref[...] = jnp.zeros_like(line_ref)
    my_place = place_ref[0]
    lag = lax.broadcasted_iota(jnp.int32, (LANES, SPAN), 1) - lax.broadcasted_iota(jnp.int32, (LANES, SPAN), 0)
    contract = (((1,), (1,)), ((), ()))

    def one(step, carry):
        entry = entry_ref[step]
        row = row_ref[entry]
        shift = shift_ref[entry]
        skip, fine = shift // LANES, shift % LANES
        for tile in range(blocks + KW - 1):
            line_ref[tile : tile + 1, :] = series_ref[skip + tile, pl.ds(row, 1), :]
        lines = line_ref[...]
        squares = lines * lines
        high = squares.astype(jnp.bfloat16).astype(jnp.float32)
        high_ref[...] = high
        low_ref[...] = squares - high
        def windows(ref):
            return jnp.concatenate(
                [ref[k : k + blocks, :].astype(jnp.bfloat16) for k in range(KW)], axis=1
            )

        group = pl.multiple_of(entry // GROUP * GROUP, GROUP)
        group_ref[...] = wave_ref[pl.ds(group, GROUP), :].astype(jnp.float32)
        wave = jnp.concatenate(
            [group_ref[pl.ds(entry % GROUP, 1), :], jnp.zeros((1, SPAN - length), jnp.float32)], axis=1
        )
        power = jnp.sum(wave * wave, axis=1, keepdims=True)
        base = pltpu.roll(jnp.broadcast_to(wave, (8, SPAN)), fine, 1)
        banded = pltpu.roll(
            jnp.concatenate([base] * (LANES // 8), axis=0), 0, 1, stride=1, stride_axis=0
        ).astype(jnp.bfloat16)
        inside = (lag >= fine) & (lag < fine + length)
        mask = jnp.where(inside, 1.0, 0.0).astype(jnp.bfloat16)
        product = lax.dot_general(windows(line_ref), banded, contract, preferred_element_type=jnp.float32)
        energy = lax.dot_general(
            windows(high_ref), mask, contract, preferred_element_type=jnp.float32
        ) + lax.dot_general(windows(low_ref), mask, contract, preferred_element_type=jnp.float32)
        scale = (energy / length + EPSILON) * (power / length + EPSILON)
        normalized = product / length / jnp.sqrt(scale)
        template = entry % out_ref.shape[1]
        for block in range(blocks):
            at = (place_of(block, bits) ^ my_place, pl.ds(template, 1), slice(None))
            out_ref[at] = out_ref[at] + normalized[block : block + 1, :]
        return carry

    lax.fori_loop(0, count_ref[0], one, 0)


VMEM_SPEC = pl.BlockSpec(memory_space=pltpu.VMEM)
SMEM_SPEC = pl.BlockSpec(memory_space=pltpu.SMEM)
HBM_SPEC = pl.BlockSpec(memory_space=pltpu.HBM)


def kernel_call(
    body, scalars, arrays, outs, scratch, flops, moved, vmem, out_specs=VMEM_SPEC, in_specs=None
):
    return pl.pallas_call(
        body,
        out_shape=outs,
        in_specs=[SMEM_SPEC] * len(scalars) + (in_specs or [VMEM_SPEC] * len(arrays)),
        out_specs=out_specs,
        scratch_shapes=scratch,
        compiler_params=pltpu.CompilerParams(vmem_limit_bytes=vmem * MIB),
        cost_estimate=pl.CostEstimate(flops=flops, bytes_accessed=moved, transcendentals=0),
    )(*scalars, *arrays)


def halve(partial, bit, count):
    half = partial.shape[0] // 2
    pairs = [(i, i ^ (1 << bit)) for i in range(count)]
    return partial[:half] + lax.ppermute(partial[half:], "stn", pairs)


def exchange(partial, bits, count):
    parts = 1 << len(bits)
    partial = partial.reshape((parts, partial.shape[0] // parts) + partial.shape[1:])
    total = partial[0]
    for part in range(1, parts):
        mask = sum(1 << bit for at, bit in enumerate(bits) if part >> (len(bits) - 1 - at) & 1)
        total = total + lax.ppermute(partial[part], "stn", [(i, i ^ mask) for i in range(count)])
    return total


def owned_entries(slots, template_channels):
    flat = template_channels.reshape(-1)
    count = flat.shape[0]
    match = (flat[None, :] == slots[:, None]).astype(jnp.int32)
    row = jnp.sum(match * jnp.arange(slots.shape[0], dtype=jnp.int32)[:, None], axis=0)
    here = jnp.sum(match, axis=0)
    number = jnp.arange(count, dtype=jnp.int32)
    before = jnp.sum(jnp.where(number[None, :] < number[:, None], here[None, :], 0), axis=1)
    where_to = jnp.where(here > 0, before, count)
    entries = jnp.sum(jnp.where(where_to[None, :] == number[:, None], number[None, :], 0), axis=1)
    return entries, row, jnp.sum(here).reshape(1)


def shards(archive, slot_of_row, templates, template_channels, moveouts, *, sizes):
    stations = lax.axis_size("stn")
    my_index = lax.axis_index("stn")
    which = lax.axis_index("tpl").astype(jnp.int32)
    rows, samples = archive.shape
    half = rows // 2
    local_templates, channels, length = templates.shape
    tiles = stations // 2
    tail_tiles = (samples // LANES - 2 * tiles) // 2
    block_lines = half + 2 * tail_tiles + 8
    f32, bf16, i32 = jnp.float32, jnp.bfloat16, jnp.int32
    shape = jax.ShapeDtypeStruct

    packed = kernel_call(
        functools.partial(pack_kernel, rows=rows, tiles=tiles, tail_tiles=tail_tiles),
        (which.reshape(1),),
        (slot_of_row.reshape(1, rows), archive),
        shape((stations, block_lines, LANES), bf16),
        [
            pltpu.VMEM((rows, (tiles + tail_tiles) * LANES), bf16),
            pltpu.VMEM((stations, block_lines, LANES), bf16),
            pltpu.VMEM((stations * 2 * tail_tiles, LANES), f32),
            pltpu.VMEM((8, LANES), i32),
            pltpu.SMEM((8, LANES), i32),
            pltpu.SemaphoreType.DMA((PARTS + 1,)),
            pltpu.SemaphoreType.DMA((PARTS,)),
            pltpu.SemaphoreType.DMA,
        ],
        4_000_000, 4_000_000, 56, HBM_SPEC, [VMEM_SPEC, HBM_SPEC],
    )
    packed, later_archive = lax.optimization_barrier((packed, archive))
    first = lax.all_to_all(packed, "stn", 0, 0, tiled=True)

    entries, entry_row, entry_count = owned_entries(slot_of_row, template_channels.T)
    waves = templates.transpose(1, 0, 2).reshape(-1, length)
    padded = samples // LANES + 8
    bits = halving_bits(sizes)
    my_place = place_of(my_index.astype(i32), bits).reshape(1)
    partial = kernel_call(
        functools.partial(correlate_kernel, length=length, bits=bits),
        (entry_count, entries, entry_row, moveouts.T.reshape(-1), my_place),
        (later_archive, waves),
        shape((stations, local_templates, LANES), f32),
        [
            pltpu.VMEM((padded, rows, LANES), f32),
            pltpu.VMEM((LANES + 8, LANES), f32),
            pltpu.VMEM((LANES + 8, LANES), f32),
            pltpu.VMEM((LANES + 8, LANES), f32),
            pltpu.VMEM((GROUP, length), f32),
        ],
        1000, 1000, 28,
    )
    for bit in bits[:EARLY]:
        partial = halve(partial, bit, stations)
    first, partial = lax.optimization_barrier((first, partial))
    partial = halve(partial, bits[EARLY], stations)

    lines, tail_rows = kernel_call(
        functools.partial(permute_kernel, rows=rows, tail_tiles=tail_tiles),
        (my_index.astype(i32).reshape(1),),
        (first,),
        (shape((stations, 2, half, LANES), bf16), shape((rows, tail_tiles * LANES), bf16)),
        [
            pltpu.VMEM((stations, half, LANES), bf16),
            pltpu.VMEM((stations * rows, LANES), f32),
            pltpu.VMEM((stations * rows, LANES), f32),
            pltpu.VMEM((stations * 2 * tail_tiles, LANES), f32),
            pltpu.VMEM((tail_tiles, rows + 8, LANES), f32),
            pltpu.VMEM((stations, LANES), f32),
            pltpu.VMEM((stations, LANES), i32),
            pltpu.SMEM((stations, LANES), i32),
            pltpu.SemaphoreType.DMA((PARTS,)),
            pltpu.SemaphoreType.DMA((2, PARTS)),
        ],
        4_000_000, 30_000_000, 52, (HBM_SPEC, VMEM_SPEC),
    )
    lines, _ = lax.optimization_barrier((lines, partial))
    lines = lines.reshape(2 * stations, half, LANES)
    second = lax.all_to_all(lines, ("stn", "tpl"), 0, 0, tiled=True)
    tail_other = lax.ppermute(tail_rows, "tpl", [(0, 1), (1, 0)])
    partial = exchange(partial, bits[EARLY + 1 : -2], stations)
    partial, tail_other = lax.optimization_barrier((partial, tail_other))
    partial = exchange(partial, bits[-2:], stations)
    stack = partial[0] * math.sqrt(length / channels)
    tail_low = jnp.where(which == 0, tail_rows, tail_other)
    tail_high = jnp.where(which == 0, tail_other, tail_rows)
    grouped = kernel_call(
        functools.partial(assemble_kernel, tiles=tiles),
        (),
        (second, tail_low, tail_high),
        shape((rows, samples), bf16),
        [pltpu.VMEM((rows, samples), bf16), pltpu.SemaphoreType.DMA((5,))],
        4_000_000, 6_000_000, 12, HBM_SPEC,
    )
    return grouped, stack


def solution(mesh):
    sizes = (2, 8, 4, 2)
    in_specs = (P("stn", None), P("stn"), P("tpl", None, None), P("tpl", None), P("tpl", None))
    out_specs = (P("stn", None), P("tpl", "stn"))
    return jax.shard_map(
        functools.partial(shards, sizes=sizes), mesh=mesh, in_specs=in_specs, out_specs=out_specs, check_vma=False
    )
```

```python
import functools
import math

import jax
import jax.numpy as jnp
from jax import lax
from jax.experimental import pallas as pl
from jax.experimental.pallas import tpu as pltpu
from jax.sharding import PartitionSpec as P

EPSILON = 1e-06
LANES = 128
KW = 7
SPAN = KW * LANES
MIB = 1024 * 1024
PARTS = 4
GROUP = 16
EARLY = 2
BESIDE = 4


def roll_half(x):
    return pltpu.roll(x, LANES // 2, 1)


def left_lanes(rows):
    return lax.broadcasted_iota(jnp.int32, (rows, LANES), 1) < LANES // 2


def send_part(source, target, part, size, sem):
    at = pl.ds(part * size, size)
    copy = pltpu.make_async_copy(source.at[at], target.at[at], sem)
    copy.start()
    return copy


def pack_kernel(
    half_ref, slot_ref, archive_hbm, out_hbm, archive_ref, out_ref, tail_ref, base_vmem, base_ref, get_sems, sems, base_sem,
    *, rows, tiles, tail_tiles,
):
    which = half_ref[0]
    half = rows // 2
    left = left_lanes(half)
    owners = out_ref.shape[0]
    tail_lines = 2 * tail_tiles
    width, tail_width = tiles * LANES, tail_tiles * LANES

    def fetch(start, at, size, number):
        start = pl.multiple_of(start, LANES)
        copy = pltpu.make_async_copy(
            archive_hbm.at[:, pl.ds(start, size)], archive_ref.at[:, pl.ds(at, size)], get_sems.at[number]
        )
        copy.start()
        return copy

    tail_fetch = fetch(2 * width + which * tail_width, width, tail_width, PARTS)
    part_width = width // PARTS
    fetches = [fetch(which * width + part * part_width, part * part_width, part_width, part) for part in range(PARTS)]
    slots = slot_ref[...]
    target, place = slots // rows, slots % rows
    before = lax.broadcasted_iota(jnp.int32, (rows, rows), 0)
    after = lax.broadcasted_iota(jnp.int32, (rows, rows), 1)
    across = jnp.broadcast_to(target, (rows, rows))
    down = jnp.sum(jnp.where(before == after, across, 0), axis=1, keepdims=True)
    rank = jnp.sum(jnp.where((across == down) & (before < after), 1, 0), axis=0, keepdims=True)
    base_vmem[0:1, 0:rows] = target * 2 + rank
    base_copy = pltpu.make_async_copy(base_vmem, base_ref, base_sem)
    base_copy.start()
    info = jnp.concatenate([target, place + rows * rank], axis=1).astype(jnp.float32)
    info = jnp.broadcast_to(info, (8, LANES))
    tail_ref[...] = jnp.zeros_like(tail_ref)
    tail_fetch.wait()
    base_copy.wait()
    for tile in range(tail_tiles):
        at = width + tile * LANES
        block = archive_ref[:, at : at + LANES].astype(jnp.float32)
        for row in range(rows):
            tail_ref[pl.ds(base_ref[0, row] * tail_tiles + tile, 1), :] = block[row : row + 1, :]

    def one(tile, carry):
        at = pl.multiple_of(tile * LANES, LANES)
        block = archive_ref[:, pl.ds(at, LANES)].astype(jnp.float32)
        upper, lower = block[:half], block[half:]
        even = jnp.where(left, upper, roll_half(lower))
        odd = jnp.where(left, roll_half(upper), lower)
        for side, lines in ((0, even), (1, odd)):
            owner = 2 * tile + side
            tail = tail_ref[pl.ds(pl.multiple_of(owner * tail_lines, 8), tail_lines), :]
            out_ref[owner] = jnp.concatenate([lines, tail, info], axis=0).astype(jnp.bfloat16)
        return carry

    copies = []
    for part in range(PARTS):
        fetches[part].wait()
        lax.fori_loop(part * tiles // PARTS, (part + 1) * tiles // PARTS, one, 0, unroll=8)
        copies.append(send_part(out_ref, out_hbm, part, owners // PARTS, sems.at[part]))
    for copy in copies:
        copy.wait()


def permute_kernel(
    owner_ref, got_ref, out_hbm, tail_out_ref,
    out_ref, plain_ref, placed_ref, tail_ref, tail_rows_ref, info_ref, route_ref, route_smem, route_sems, sems,
    *, rows, tail_tiles,
):
    stations = got_ref.shape[0]
    half = rows // 2
    left = left_lanes(half)
    tail_lines = 2 * tail_tiles

    def note(station, carry):
        info_ref[pl.ds(station, 1), :] = got_ref[station][half + tail_lines : half + tail_lines + 8].astype(
            jnp.float32
        )[:1]
        return carry

    lax.fori_loop(0, stations, note, 0, unroll=8)
    info = info_ref[...].astype(jnp.int32)
    other = pltpu.roll(info_ref[...], rows, 1).astype(jnp.int32)
    on_left = lax.broadcasted_iota(jnp.int32, info.shape, 1) < rows
    target = jnp.where(on_left, info, other)
    packed = jnp.where(on_left, other, info)
    place, rank = packed % rows, packed // rows
    mine = target == owner_ref[0]
    first = jnp.max(jnp.where(mine & (rank == 0), place, -1), axis=1, keepdims=True)
    second = jnp.max(jnp.where(mine & (rank == 1), place, -1), axis=1, keepdims=True)
    lane = lax.broadcasted_iota(jnp.int32, info.shape, 1)
    kept = jnp.where(lane == rows, first, second)
    kept = jnp.where(kept < 0, rows, kept)
    route_ref[...] = jnp.where(on_left, target * rows + place, kept)
    share = stations // PARTS
    route_copies = [send_part(route_ref, route_smem, part, share, route_sems.at[part]) for part in range(PARTS)]

    def expand(station, carry):
        block = got_ref[station].astype(jnp.float32)
        lines = block[:half]
        at = pl.multiple_of(station * rows, 8)
        plain_ref[pl.ds(at, half), :] = lines
        plain_ref[pl.ds(at + half, half), :] = roll_half(lines)
        tail_ref[pl.ds(pl.multiple_of(station * tail_lines, 8), tail_lines), :] = block[half : half + tail_lines]
        return carry

    lax.fori_loop(0, stations, expand, 0, unroll=8)

    def move(station, carry):
        lines = plain_ref[pl.ds(pl.multiple_of(station * rows, 8), rows), :]
        for row in range(rows):
            placed_ref[pl.ds(route_smem[station, row], 1), :] = lines[row : row + 1, :]
        return carry

    for part in range(PARTS):
        route_copies[part].wait()
        lax.fori_loop(part * share, (part + 1) * share, move, 0, unroll=4)

    def join(station, carry):
        at = pl.multiple_of(station * rows, 8)
        lines = jnp.where(left, placed_ref[pl.ds(at, half), :], roll_half(placed_ref[pl.ds(at + half, half), :]))
        out_ref[station] = lines.astype(jnp.bfloat16)
        return carry

    copies = []
    for part in range(PARTS):
        lax.fori_loop(part * stations // PARTS, (part + 1) * stations // PARTS, join, 0, unroll=16)
        for which in range(2):
            copies.append(
                send_part(out_ref, out_hbm.at[:, which], part, stations // PARTS, sems.at[which, part])
            )
    def keep(station, carry):
        for rank in range(2):
            row = route_smem[station, rows + rank]
            for tile in range(tail_tiles):
                line = station * tail_lines + rank * tail_tiles + tile
                tail_rows_ref[tile, pl.ds(row, 1), :] = tail_ref[pl.ds(line, 1), :]
        return carry

    lax.fori_loop(0, stations, keep, 0, unroll=8)
    for tile in range(tail_tiles):
        tail_out_ref[:, tile * LANES : (tile + 1) * LANES] = tail_rows_ref[tile, :rows, :].astype(jnp.bfloat16)
    for copy in copies:
        copy.wait()


def assemble_kernel(got_ref, tail_low_ref, tail_high_ref, out_hbm, out_ref, sems, *, tiles):
    half = got_ref.shape[1]
    left = left_lanes(half)
    copies = []

    def send(start, size):
        at = (slice(None), pl.ds(start, size))
        copies.append(pltpu.make_async_copy(out_ref.at[at], out_hbm.at[at], sems.at[len(copies)]))
        copies[-1].start()

    at = 2 * tiles * LANES
    width = tail_low_ref.shape[1]
    out_ref[:, at : at + width] = tail_low_ref[...]
    out_ref[:, at + width : at + 2 * width] = tail_high_ref[...]
    send(at, 2 * width)
    for which in range(2):

        def one(tile, carry, which=which):
            even = got_ref[4 * tile + which].astype(jnp.float32)
            odd = got_ref[4 * tile + 2 + which].astype(jnp.float32)
            upper = jnp.where(left, even, roll_half(odd))
            lower = jnp.where(left, roll_half(even), odd)
            at = pl.multiple_of((which * tiles + tile) * LANES, LANES)
            out_ref[:, pl.ds(at, LANES)] = jnp.concatenate([upper, lower], axis=0).astype(jnp.bfloat16)
            return carry

        part = tiles // 2
        for start in range(0, tiles, part):
            lax.fori_loop(start, start + part, one, 0, unroll=8)
            send((which * tiles + start) * LANES, part * LANES)
    for copy in copies:
        copy.wait()


def halving_bits(sizes):
    ys, zs, xs, cores = (size.bit_length() - 1 for size in sizes)
    x_from, z_from, y_from = cores, cores + xs, cores + xs + zs
    return (
        list(range(cores))
        + list(range(y_from, y_from + ys))
        + list(range(z_from, y_from - 1))
        + list(range(x_from, z_from))
        + [y_from - 1]
    )


def place_of(index, bits):
    place = 0
    for at, bit in enumerate(bits):
        place = place + ((index >> bit) & 1) * (1 << (len(bits) - 1 - at))
    return place


def correlate_kernel(
    count_ref, entry_ref, row_ref, shift_ref, place_ref, archive_ref, wave_ref, out_ref,
    series_ref, line_ref, high_ref, low_ref, group_ref, *, length, bits,
):
    rows = archive_ref.shape[0]
    tiles = archive_ref.shape[1] // LANES
    blocks = LANES
    padded = series_ref.shape[0]

    def widen(tile, carry):
        at = pl.multiple_of(tile * LANES, LANES)
        series_ref[tile] = archive_ref[:, pl.ds(at, LANES)].astype(jnp.float32)
        return carry

    lax.fori_loop(0, tiles, widen, 0, unroll=8)
    for tile in range(tiles, padded):
        series_ref[tile] = jnp.zeros((rows, LANES), jnp.float32)
    out_ref[...] = jnp.zeros_like(out_ref)
    line_ref[...] = jnp.zeros_like(line_ref)
    my_place = place_ref[0]
    lag = lax.broadcasted_iota(jnp.int32, (LANES, SPAN), 1) - lax.broadcasted_iota(jnp.int32, (LANES, SPAN), 0)
    contract = (((1,), (1,)), ((), ()))

    def one(step, carry):
        entry = entry_ref[step]
        row = row_ref[entry]
        shift = shift_ref[entry]
        skip, fine = shift // LANES, shift % LANES
        for tile in range(blocks + KW - 1):
            line_ref[tile : tile + 1, :] = series_ref[skip + tile, pl.ds(row, 1), :]
        lines = line_ref[...]
        squares = lines * lines
        high = squares.astype(jnp.bfloat16).astype(jnp.float32)
        high_ref[...] = high
        low_ref[...] = squares - high
        def windows(ref):
            return jnp.concatenate(
                [ref[k : k + blocks, :].astype(jnp.bfloat16) for k in range(KW)], axis=1
            )

        group = pl.multiple_of(entry // GROUP * GROUP, GROUP)
        group_ref[...] = wave_ref[pl.ds(group, GROUP), :].astype(jnp.float32)
        wave = jnp.concatenate(
            [group_ref[pl.ds(entry % GROUP, 1), :], jnp.zeros((1, SPAN - length), jnp.float32)], axis=1
        )
        power = jnp.sum(wave * wave, axis=1, keepdims=True)
        base = pltpu.roll(jnp.broadcast_to(wave, (8, SPAN)), fine, 1)
        banded = pltpu.roll(
            jnp.concatenate([base] * (LANES // 8), axis=0), 0, 1, stride=1, stride_axis=0
        ).astype(jnp.bfloat16)
        inside = (lag >= fine) & (lag < fine + length)
        mask = jnp.where(inside, 1.0, 0.0).astype(jnp.bfloat16)
        product = lax.dot_general(windows(line_ref), banded, contract, preferred_element_type=jnp.float32)
        energy = lax.dot_general(
            windows(high_ref), mask, contract, preferred_element_type=jnp.float32
        ) + lax.dot_general(windows(low_ref), mask, contract, preferred_element_type=jnp.float32)
        scale = (energy / length + EPSILON) * (power / length + EPSILON)
        normalized = product / length / jnp.sqrt(scale)
        template = entry % out_ref.shape[1]
        for block in range(blocks):
            at = (place_of(block, bits) ^ my_place, pl.ds(template, 1), slice(None))
            out_ref[at] = out_ref[at] + normalized[block : block + 1, :]
        return carry

    lax.fori_loop(0, count_ref[0], one, 0)


VMEM_SPEC = pl.BlockSpec(memory_space=pltpu.VMEM)
SMEM_SPEC = pl.BlockSpec(memory_space=pltpu.SMEM)
HBM_SPEC = pl.BlockSpec(memory_space=pltpu.HBM)


def kernel_call(
    body, scalars, arrays, outs, scratch, flops, moved, vmem, out_specs=VMEM_SPEC, in_specs=None
):
    return pl.pallas_call(
        body,
        out_shape=outs,
        in_specs=[SMEM_SPEC] * len(scalars) + (in_specs or [VMEM_SPEC] * len(arrays)),
        out_specs=out_specs,
        scratch_shapes=scratch,
        compiler_params=pltpu.CompilerParams(vmem_limit_bytes=vmem * MIB),
        cost_estimate=pl.CostEstimate(flops=flops, bytes_accessed=moved, transcendentals=0),
    )(*scalars, *arrays)


def halve(partial, bit, count):
    half = partial.shape[0] // 2
    pairs = [(i, i ^ (1 << bit)) for i in range(count)]
    return partial[:half] + lax.ppermute(partial[half:], "stn", pairs)


def exchange(partial, bits, count):
    parts = 1 << len(bits)
    partial = partial.reshape((parts, partial.shape[0] // parts) + partial.shape[1:])
    total = partial[0]
    for part in range(1, parts):
        mask = sum(1 << bit for at, bit in enumerate(bits) if part >> (len(bits) - 1 - at) & 1)
        total = total + lax.ppermute(partial[part], "stn", [(i, i ^ mask) for i in range(count)])
    return total


def owned_entries(slots, template_channels):
    flat = template_channels.reshape(-1)
    count = flat.shape[0]
    match = (flat[None, :] == slots[:, None]).astype(jnp.int32)
    row = jnp.sum(match * jnp.arange(slots.shape[0], dtype=jnp.int32)[:, None], axis=0)
    here = jnp.sum(match, axis=0)
    number = jnp.arange(count, dtype=jnp.int32)
    before = jnp.sum(jnp.where(number[None, :] < number[:, None], here[None, :], 0), axis=1)
    where_to = jnp.where(here > 0, before, count)
    entries = jnp.sum(jnp.where(where_to[None, :] == number[:, None], number[None, :], 0), axis=1)
    return entries, row, jnp.sum(here).reshape(1)


def shards(archive, slot_of_row, templates, template_channels, moveouts, *, sizes):
    stations = lax.axis_size("stn")
    my_index = lax.axis_index("stn")
    which = lax.axis_index("tpl").astype(jnp.int32)
    rows, samples = archive.shape
    half = rows // 2
    local_templates, channels, length = templates.shape
    tiles = stations // 2
    tail_tiles = (samples // LANES - 2 * tiles) // 2
    block_lines = half + 2 * tail_tiles + 8
    f32, bf16, i32 = jnp.float32, jnp.bfloat16, jnp.int32
    shape = jax.ShapeDtypeStruct

    packed = kernel_call(
        functools.partial(pack_kernel, rows=rows, tiles=tiles, tail_tiles=tail_tiles),
        (which.reshape(1),),
        (slot_of_row.reshape(1, rows), archive),
        shape((stations, block_lines, LANES), bf16),
        [
            pltpu.VMEM((rows, (tiles + tail_tiles) * LANES), bf16),
            pltpu.VMEM((stations, block_lines, LANES), bf16),
            pltpu.VMEM((stations * 2 * tail_tiles, LANES), f32),
            pltpu.VMEM((8, LANES), i32),
            pltpu.SMEM((8, LANES), i32),
            pltpu.SemaphoreType.DMA((PARTS + 1,)),
            pltpu.SemaphoreType.DMA((PARTS,)),
            pltpu.SemaphoreType.DMA,
        ],
        4_000_000, 4_000_000, 56, HBM_SPEC, [VMEM_SPEC, HBM_SPEC],
    )
    packed, later_archive = lax.optimization_barrier((packed, archive))
    first = lax.all_to_all(packed, "stn", 0, 0, tiled=True)

    entries, entry_row, entry_count = owned_entries(slot_of_row, template_channels.T)
    waves = templates.transpose(1, 0, 2).reshape(-1, length)
    padded = samples // LANES + 8
    bits = halving_bits(sizes)
    my_place = place_of(my_index.astype(i32), bits).reshape(1)
    partial = kernel_call(
        functools.partial(correlate_kernel, length=length, bits=bits),
        (entry_count, entries, entry_row, moveouts.T.reshape(-1), my_place),
        (later_archive, waves),
        shape((stations, local_templates, LANES), f32),
        [
            pltpu.VMEM((padded, rows, LANES), f32),
            pltpu.VMEM((LANES + 8, LANES), f32),
            pltpu.VMEM((LANES + 8, LANES), f32),
            pltpu.VMEM((LANES + 8, LANES), f32),
            pltpu.VMEM((GROUP, length), f32),
        ],
        1000, 1000, 28,
    )
    for bit in bits[:EARLY]:
        partial = halve(partial, bit, stations)
    first, partial = lax.optimization_barrier((first, partial))
    partial = exchange(partial, bits[EARLY:BESIDE], stations)

    lines, tail_rows = kernel_call(
        functools.partial(permute_kernel, rows=rows, tail_tiles=tail_tiles),
        (my_index.astype(i32).reshape(1),),
        (first,),
        (shape((stations, 2, half, LANES), bf16), shape((rows, tail_tiles * LANES), bf16)),
        [
            pltpu.VMEM((stations, half, LANES), bf16),
            pltpu.VMEM((stations * rows, LANES), f32),
            pltpu.VMEM((stations * rows, LANES), f32),
            pltpu.VMEM((stations * 2 * tail_tiles, LANES), f32),
            pltpu.VMEM((tail_tiles, rows + 8, LANES), f32),
            pltpu.VMEM((stations, LANES), f32),
            pltpu.VMEM((stations, LANES), i32),
            pltpu.SMEM((stations, LANES), i32),
            pltpu.SemaphoreType.DMA((PARTS,)),
            pltpu.SemaphoreType.DMA((2, PARTS)),
        ],
        4_000_000, 30_000_000, 52, (HBM_SPEC, VMEM_SPEC),
    )
    lines, _ = lax.optimization_barrier((lines, partial))
    lines = lines.reshape(2 * stations, half, LANES)
    second = lax.all_to_all(lines, ("stn", "tpl"), 0, 0, tiled=True)
    tail_other = lax.ppermute(tail_rows, "tpl", [(0, 1), (1, 0)])
    partial = exchange(partial, bits[BESIDE:-1], stations)
    partial, tail_other = lax.optimization_barrier((partial, tail_other))
    partial = halve(partial, bits[-1], stations)
    stack = partial[0] * math.sqrt(length / channels)
    tail_low = jnp.where(which == 0, tail_rows, tail_other)
    tail_high = jnp.where(which == 0, tail_other, tail_rows)
    grouped = kernel_call(
        functools.partial(assemble_kernel, tiles=tiles),
        (),
        (second, tail_low, tail_high),
        shape((rows, samples), bf16),
        [pltpu.VMEM((rows, samples), bf16), pltpu.SemaphoreType.DMA((5,))],
        4_000_000, 6_000_000, 12, HBM_SPEC,
    )
    return grouped, stack


def solution(mesh):
    sizes = (2, 8, 4, 2)
    in_specs = (P("stn", None), P("stn"), P("tpl", None, None), P("tpl", None), P("tpl", None))
    out_specs = (P("stn", None), P("tpl", "stn"))
    return jax.shard_map(
        functools.partial(shards, sizes=sizes), mesh=mesh, in_specs=in_specs, out_specs=out_specs, check_vma=False
    )
```

```python
import functools
import math

import jax
import jax.numpy as jnp
from jax import lax
from jax.experimental import pallas as pl
from jax.experimental.pallas import tpu as pltpu
from jax.sharding import PartitionSpec as P

EPSILON = 1e-06
LANES = 128
KW = 7
SPAN = KW * LANES
MIB = 1024 * 1024
PARTS = 8
GROUP = 16
EARLY = 2


def roll_half(x):
    return pltpu.roll(x, LANES // 2, 1)


def left_lanes(rows):
    return lax.broadcasted_iota(jnp.int32, (rows, LANES), 1) < LANES // 2


def send_part(source, target, part, size, sem):
    at = pl.ds(part * size, size)
    copy = pltpu.make_async_copy(source.at[at], target.at[at], sem)
    copy.start()
    return copy


def pack_kernel(
    half_ref, slot_ref, archive_hbm, out_hbm, archive_ref, out_ref, tail_ref, base_vmem, base_ref, get_sems, sems, base_sem,
    *, rows, tiles, tail_tiles,
):
    which = half_ref[0]
    half = rows // 2
    left = left_lanes(half)
    owners = out_ref.shape[0]
    tail_lines = 2 * tail_tiles
    width, tail_width = tiles * LANES, tail_tiles * LANES

    def fetch(start, at, size, number):
        start = pl.multiple_of(start, LANES)
        copy = pltpu.make_async_copy(
            archive_hbm.at[:, pl.ds(start, size)], archive_ref.at[:, pl.ds(at, size)], get_sems.at[number]
        )
        copy.start()
        return copy

    tail_fetch = fetch(2 * width + which * tail_width, width, tail_width, PARTS)
    part_width = width // PARTS
    fetches = [fetch(which * width + part * part_width, part * part_width, part_width, part) for part in range(PARTS)]
    slots = slot_ref[...]
    target, place = slots // rows, slots % rows
    before = lax.broadcasted_iota(jnp.int32, (rows, rows), 0)
    after = lax.broadcasted_iota(jnp.int32, (rows, rows), 1)
    across = jnp.broadcast_to(target, (rows, rows))
    down = jnp.sum(jnp.where(before == after, across, 0), axis=1, keepdims=True)
    rank = jnp.sum(jnp.where((across == down) & (before < after), 1, 0), axis=0, keepdims=True)
    base_vmem[0:1, 0:rows] = target * 2 + rank
    base_copy = pltpu.make_async_copy(base_vmem, base_ref, base_sem)
    base_copy.start()
    info = jnp.concatenate([target, place + rows * rank], axis=1).astype(jnp.float32)
    info = jnp.broadcast_to(info, (8, LANES))
    tail_ref[...] = jnp.zeros_like(tail_ref)
    tail_fetch.wait()
    base_copy.wait()
    for tile in range(tail_tiles):
        at = width + tile * LANES
        block = archive_ref[:, at : at + LANES].astype(jnp.float32)
        for row in range(rows):
            tail_ref[pl.ds(base_ref[0, row] * tail_tiles + tile, 1), :] = block[row : row + 1, :]

    def one(tile, carry):
        at = pl.multiple_of(tile * LANES, LANES)
        block = archive_ref[:, pl.ds(at, LANES)].astype(jnp.float32)
        upper, lower = block[:half], block[half:]
        even = jnp.where(left, upper, roll_half(lower))
        odd = jnp.where(left, roll_half(upper), lower)
        for side, lines in ((0, even), (1, odd)):
            owner = 2 * tile + side
            tail = tail_ref[pl.ds(pl.multiple_of(owner * tail_lines, 8), tail_lines), :]
            out_ref[owner] = jnp.concatenate([lines, tail, info], axis=0).astype(jnp.bfloat16)
        return carry

    copies = []
    for part in range(PARTS):
        fetches[part].wait()
        lax.fori_loop(part * tiles // PARTS, (part + 1) * tiles // PARTS, one, 0, unroll=8)
        copies.append(send_part(out_ref, out_hbm, part, owners // PARTS, sems.at[part]))
    for copy in copies:
        copy.wait()


def permute_kernel(
    owner_ref, got_ref, out_hbm, tail_out_ref,
    out_ref, plain_ref, placed_ref, tail_ref, tail_rows_ref, info_ref, route_ref, route_smem, route_sems, sems,
    *, rows, tail_tiles,
):
    stations = got_ref.shape[0]
    half = rows // 2
    left = left_lanes(half)
    tail_lines = 2 * tail_tiles

    def note(station, carry):
        info_ref[pl.ds(station, 1), :] = got_ref[station][half + tail_lines : half + tail_lines + 8].astype(
            jnp.float32
        )[:1]
        return carry

    lax.fori_loop(0, stations, note, 0, unroll=8)
    info = info_ref[...].astype(jnp.int32)
    other = pltpu.roll(info_ref[...], rows, 1).astype(jnp.int32)
    on_left = lax.broadcasted_iota(jnp.int32, info.shape, 1) < rows
    target = jnp.where(on_left, info, other)
    packed = jnp.where(on_left, other, info)
    place, rank = packed % rows, packed // rows
    mine = target == owner_ref[0]
    first = jnp.max(jnp.where(mine & (rank == 0), place, -1), axis=1, keepdims=True)
    second = jnp.max(jnp.where(mine & (rank == 1), place, -1), axis=1, keepdims=True)
    lane = lax.broadcasted_iota(jnp.int32, info.shape, 1)
    kept = jnp.where(lane == rows, first, second)
    kept = jnp.where(kept < 0, rows, kept)
    route_ref[...] = jnp.where(on_left, target * rows + place, kept)
    share = stations // PARTS
    route_copies = [send_part(route_ref, route_smem, part, share, route_sems.at[part]) for part in range(PARTS)]

    def expand(station, carry):
        block = got_ref[station].astype(jnp.float32)
        lines = block[:half]
        at = pl.multiple_of(station * rows, 8)
        plain_ref[pl.ds(at, half), :] = lines
        plain_ref[pl.ds(at + half, half), :] = roll_half(lines)
        tail_ref[pl.ds(pl.multiple_of(station * tail_lines, 8), tail_lines), :] = block[half : half + tail_lines]
        return carry

    lax.fori_loop(0, stations, expand, 0, unroll=8)

    def move(station, carry):
        lines = plain_ref[pl.ds(pl.multiple_of(station * rows, 8), rows), :]
        for row in range(rows):
            placed_ref[pl.ds(route_smem[station, row], 1), :] = lines[row : row + 1, :]
        return carry

    for part in range(PARTS):
        route_copies[part].wait()
        lax.fori_loop(part * share, (part + 1) * share, move, 0, unroll=4)

    def join(station, carry):
        at = pl.multiple_of(station * rows, 8)
        lines = jnp.where(left, placed_ref[pl.ds(at, half), :], roll_half(placed_ref[pl.ds(at + half, half), :]))
        out_ref[station] = lines.astype(jnp.bfloat16)
        return carry

    copies = []
    for part in range(PARTS):
        lax.fori_loop(part * stations // PARTS, (part + 1) * stations // PARTS, join, 0, unroll=16)
        for which in range(2):
            copies.append(
                send_part(out_ref, out_hbm.at[:, which], part, stations // PARTS, sems.at[which, part])
            )
    def keep(station, carry):
        for rank in range(2):
            row = route_smem[station, rows + rank]
            for tile in range(tail_tiles):
                line = station * tail_lines + rank * tail_tiles + tile
                tail_rows_ref[tile, pl.ds(row, 1), :] = tail_ref[pl.ds(line, 1), :]
        return carry

    lax.fori_loop(0, stations, keep, 0, unroll=8)
    for tile in range(tail_tiles):
        tail_out_ref[:, tile * LANES : (tile + 1) * LANES] = tail_rows_ref[tile, :rows, :].astype(jnp.bfloat16)
    for copy in copies:
        copy.wait()


def assemble_kernel(got_ref, tail_low_ref, tail_high_ref, out_hbm, out_ref, sems, *, tiles):
    half = got_ref.shape[1]
    left = left_lanes(half)
    copies = []

    def send(start, size):
        at = (slice(None), pl.ds(start, size))
        copies.append(pltpu.make_async_copy(out_ref.at[at], out_hbm.at[at], sems.at[len(copies)]))
        copies[-1].start()

    at = 2 * tiles * LANES
    width = tail_low_ref.shape[1]
    out_ref[:, at : at + width] = tail_low_ref[...]
    out_ref[:, at + width : at + 2 * width] = tail_high_ref[...]
    send(at, 2 * width)
    for which in range(2):

        def one(tile, carry, which=which):
            even = got_ref[4 * tile + which].astype(jnp.float32)
            odd = got_ref[4 * tile + 2 + which].astype(jnp.float32)
            upper = jnp.where(left, even, roll_half(odd))
            lower = jnp.where(left, roll_half(even), odd)
            at = pl.multiple_of((which * tiles + tile) * LANES, LANES)
            out_ref[:, pl.ds(at, LANES)] = jnp.concatenate([upper, lower], axis=0).astype(jnp.bfloat16)
            return carry

        part = tiles // 2
        for start in range(0, tiles, part):
            lax.fori_loop(start, start + part, one, 0, unroll=8)
            send((which * tiles + start) * LANES, part * LANES)
    for copy in copies:
        copy.wait()


def halving_bits(sizes):
    ys, zs, xs, cores = (size.bit_length() - 1 for size in sizes)
    x_from, z_from, y_from = cores, cores + xs, cores + xs + zs
    return (
        list(range(cores))
        + list(range(y_from, y_from + ys))
        + [z_from]
        + list(range(x_from, z_from))
        + list(reversed(range(z_from + 1, y_from)))
    )


def place_of(index, bits):
    place = 0
    for at, bit in enumerate(bits):
        place = place + ((index >> bit) & 1) * (1 << (len(bits) - 1 - at))
    return place


def correlate_kernel(
    count_ref, entry_ref, row_ref, shift_ref, place_ref, archive_ref, wave_ref, out_ref,
    series_ref, line_ref, high_ref, low_ref, group_ref, *, length, bits,
):
    rows = archive_ref.shape[0]
    tiles = archive_ref.shape[1] // LANES
    blocks = LANES
    padded = series_ref.shape[0]

    def widen(tile, carry):
        at = pl.multiple_of(tile * LANES, LANES)
        series_ref[tile] = archive_ref[:, pl.ds(at, LANES)].astype(jnp.float32)
        return carry

    lax.fori_loop(0, tiles, widen, 0, unroll=8)
    for tile in range(tiles, padded):
        series_ref[tile] = jnp.zeros((rows, LANES), jnp.float32)
    out_ref[...] = jnp.zeros_like(out_ref)
    line_ref[...] = jnp.zeros_like(line_ref)
    my_place = place_ref[0]
    lag = lax.broadcasted_iota(jnp.int32, (LANES, SPAN), 1) - lax.broadcasted_iota(jnp.int32, (LANES, SPAN), 0)
    contract = (((1,), (1,)), ((), ()))

    def one(step, carry):
        entry = entry_ref[step]
        row = row_ref[entry]
        shift = shift_ref[entry]
        skip, fine = shift // LANES, shift % LANES
        for tile in range(blocks + KW - 1):
            line_ref[tile : tile + 1, :] = series_ref[skip + tile, pl.ds(row, 1), :]
        lines = line_ref[...]
        squares = lines * lines
        high = squares.astype(jnp.bfloat16).astype(jnp.float32)
        high_ref[...] = high
        low_ref[...] = squares - high
        def windows(ref):
            return jnp.concatenate(
                [ref[k : k + blocks, :].astype(jnp.bfloat16) for k in range(KW)], axis=1
            )

        group = pl.multiple_of(entry // GROUP * GROUP, GROUP)
        group_ref[...] = wave_ref[pl.ds(group, GROUP), :].astype(jnp.float32)
        wave = jnp.concatenate(
            [group_ref[pl.ds(entry % GROUP, 1), :], jnp.zeros((1, SPAN - length), jnp.float32)], axis=1
        )
        power = jnp.sum(wave * wave, axis=1, keepdims=True)
        base = pltpu.roll(jnp.broadcast_to(wave, (8, SPAN)), fine, 1)
        banded = pltpu.roll(
            jnp.concatenate([base] * (LANES // 8), axis=0), 0, 1, stride=1, stride_axis=0
        ).astype(jnp.bfloat16)
        inside = (lag >= fine) & (lag < fine + length)
        mask = jnp.where(inside, 1.0, 0.0).astype(jnp.bfloat16)
        product = lax.dot_general(windows(line_ref), banded, contract, preferred_element_type=jnp.float32)
        both = lax.dot_general(
            jnp.concatenate([windows(high_ref), windows(low_ref)], axis=0),
            mask, contract, preferred_element_type=jnp.float32,
        )
        energy = both[:blocks] + both[blocks:]
        scale = (energy / length + EPSILON) * (power / length + EPSILON)
        normalized = product / length / jnp.sqrt(scale)
        template = entry % out_ref.shape[1]
        for block in range(blocks):
            at = (place_of(block, bits) ^ my_place, pl.ds(template, 1), slice(None))
            out_ref[at] = out_ref[at] + normalized[block : block + 1, :]
        return carry

    lax.fori_loop(0, count_ref[0], one, 0)


VMEM_SPEC = pl.BlockSpec(memory_space=pltpu.VMEM)
SMEM_SPEC = pl.BlockSpec(memory_space=pltpu.SMEM)
HBM_SPEC = pl.BlockSpec(memory_space=pltpu.HBM)


def kernel_call(
    body, scalars, arrays, outs, scratch, flops, moved, vmem, out_specs=VMEM_SPEC, in_specs=None
):
    return pl.pallas_call(
        body,
        out_shape=outs,
        in_specs=[SMEM_SPEC] * len(scalars) + (in_specs or [VMEM_SPEC] * len(arrays)),
        out_specs=out_specs,
        scratch_shapes=scratch,
        compiler_params=pltpu.CompilerParams(vmem_limit_bytes=vmem * MIB),
        cost_estimate=pl.CostEstimate(flops=flops, bytes_accessed=moved, transcendentals=0),
    )(*scalars, *arrays)


def halve(partial, bit, count):
    half = partial.shape[0] // 2
    pairs = [(i, i ^ (1 << bit)) for i in range(count)]
    return partial[:half] + lax.ppermute(partial[half:], "stn", pairs)


def exchange(partial, bits, count):
    parts = 1 << len(bits)
    partial = partial.reshape((parts, partial.shape[0] // parts) + partial.shape[1:])
    total = partial[0]
    for part in range(1, parts):
        mask = sum(1 << bit for at, bit in enumerate(bits) if part >> (len(bits) - 1 - at) & 1)
        total = total + lax.ppermute(partial[part], "stn", [(i, i ^ mask) for i in range(count)])
    return total


def owned_entries(slots, template_channels):
    flat = template_channels.reshape(-1)
    count = flat.shape[0]
    match = (flat[None, :] == slots[:, None]).astype(jnp.int32)
    row = jnp.sum(match * jnp.arange(slots.shape[0], dtype=jnp.int32)[:, None], axis=0)
    here = jnp.sum(match, axis=0)
    number = jnp.arange(count, dtype=jnp.int32)
    before = jnp.sum(jnp.where(number[None, :] < number[:, None], here[None, :], 0), axis=1)
    where_to = jnp.where(here > 0, before, count)
    entries = jnp.sum(jnp.where(where_to[None, :] == number[:, None], number[None, :], 0), axis=1)
    return entries, row, jnp.sum(here).reshape(1)


def shards(archive, slot_of_row, templates, template_channels, moveouts, *, sizes):
    stations = lax.axis_size("stn")
    my_index = lax.axis_index("stn")
    which = lax.axis_index("tpl").astype(jnp.int32)
    rows, samples = archive.shape
    half = rows // 2
    local_templates, channels, length = templates.shape
    tiles = stations // 2
    tail_tiles = (samples // LANES - 2 * tiles) // 2
    block_lines = half + 2 * tail_tiles + 8
    f32, bf16, i32 = jnp.float32, jnp.bfloat16, jnp.int32
    shape = jax.ShapeDtypeStruct

    packed = kernel_call(
        functools.partial(pack_kernel, rows=rows, tiles=tiles, tail_tiles=tail_tiles),
        (which.reshape(1),),
        (slot_of_row.reshape(1, rows), archive),
        shape((stations, block_lines, LANES), bf16),
        [
            pltpu.VMEM((rows, (tiles + tail_tiles) * LANES), bf16),
            pltpu.VMEM((stations, block_lines, LANES), bf16),
            pltpu.VMEM((stations * 2 * tail_tiles, LANES), f32),
            pltpu.VMEM((8, LANES), i32),
            pltpu.SMEM((8, LANES), i32),
            pltpu.SemaphoreType.DMA((PARTS + 1,)),
            pltpu.SemaphoreType.DMA((PARTS,)),
            pltpu.SemaphoreType.DMA,
        ],
        4_000_000, 4_000_000, 56, HBM_SPEC, [VMEM_SPEC, HBM_SPEC],
    )
    packed, later_archive = lax.optimization_barrier((packed, archive))
    first = lax.all_to_all(packed, "stn", 0, 0, tiled=True)

    entries, entry_row, entry_count = owned_entries(slot_of_row, template_channels.T)
    waves = templates.transpose(1, 0, 2).reshape(-1, length)
    padded = samples // LANES + 8
    bits = halving_bits(sizes)
    my_place = place_of(my_index.astype(i32), bits).reshape(1)
    partial = kernel_call(
        functools.partial(correlate_kernel, length=length, bits=bits),
        (entry_count, entries, entry_row, moveouts.T.reshape(-1), my_place),
        (later_archive, waves),
        shape((stations, local_templates, LANES), f32),
        [
            pltpu.VMEM((padded, rows, LANES), f32),
            pltpu.VMEM((LANES + 8, LANES), f32),
            pltpu.VMEM((LANES + 8, LANES), f32),
            pltpu.VMEM((LANES + 8, LANES), f32),
            pltpu.VMEM((GROUP, length), f32),
        ],
        1000, 1000, 28,
    )
    for bit in bits[:EARLY]:
        partial = halve(partial, bit, stations)
    first, partial = lax.optimization_barrier((first, partial))
    partial = halve(partial, bits[EARLY], stations)

    lines, tail_rows = kernel_call(
        functools.partial(permute_kernel, rows=rows, tail_tiles=tail_tiles),
        (my_index.astype(i32).reshape(1),),
        (first,),
        (shape((stations, 2, half, LANES), bf16), shape((rows, tail_tiles * LANES), bf16)),
        [
            pltpu.VMEM((stations, half, LANES), bf16),
            pltpu.VMEM((stations * rows, LANES), f32),
            pltpu.VMEM((stations * rows, LANES), f32),
            pltpu.VMEM((stations * 2 * tail_tiles, LANES), f32),
            pltpu.VMEM((tail_tiles, rows + 8, LANES), f32),
            pltpu.VMEM((stations, LANES), f32),
            pltpu.VMEM((stations, LANES), i32),
            pltpu.SMEM((stations, LANES), i32),
            pltpu.SemaphoreType.DMA((PARTS,)),
            pltpu.SemaphoreType.DMA((2, PARTS)),
        ],
        4_000_000, 30_000_000, 52, (HBM_SPEC, VMEM_SPEC),
    )
    lines, _ = lax.optimization_barrier((lines, partial))
    lines = lines.reshape(2 * stations, half, LANES)
    second = lax.all_to_all(lines, ("stn", "tpl"), 0, 0, tiled=True)
    tail_other = lax.ppermute(tail_rows, "tpl", [(0, 1), (1, 0)])
    partial = exchange(partial, bits[EARLY + 1 : -2], stations)
    partial, tail_other = lax.optimization_barrier((partial, tail_other))
    partial = exchange(partial, bits[-2:], stations)
    stack = partial[0] * math.sqrt(length / channels)
    tail_low = jnp.where(which == 0, tail_rows, tail_other)
    tail_high = jnp.where(which == 0, tail_other, tail_rows)
    grouped = kernel_call(
        functools.partial(assemble_kernel, tiles=tiles),
        (),
        (second, tail_low, tail_high),
        shape((rows, samples), bf16),
        [pltpu.VMEM((rows, samples), bf16), pltpu.SemaphoreType.DMA((5,))],
        4_000_000, 6_000_000, 12, HBM_SPEC,
    )
    return grouped, stack


def solution(mesh):
    sizes = (2, 8, 4, 2)
    in_specs = (P("stn", None), P("stn"), P("tpl", None, None), P("tpl", None), P("tpl", None))
    out_specs = (P("stn", None), P("tpl", "stn"))
    return jax.shard_map(
        functools.partial(shards, sizes=sizes), mesh=mesh, in_specs=in_specs, out_specs=out_specs, check_vma=False
    )
```
